128 devices in a mesh: slab: 4 (over x), blk: 32 (over y, z, core).
Axes of the slice: x: 4, y: 4, z: 4, core: 2. Of those that a mesh axis runs over, the one named last changes fastest.
Arguments:
- populations: float32 [19, 128, 512, 128], P(None, 'slab', 'blk'), may hold values from 0.01 to 0.6, as said below
- solid: int32 [128, 512, 128], P('slab', 'blk'), may hold values 0 or 1
- wetting: int32 [128, 512, 128], P('slab', 'blk'), may hold values 0 or 1
- dest: int32 [4, 512], P('slab', 'blk'), may hold values from 0 to 511, as said below
Outputs:
- relocated: float32 [2048, 19, 4096], P(('slab', 'blk'))
The draws below stay inside these ranges and needn't reach their ends.
Inputs may be any that keep to these rules, and one draw needn't show every extreme that they name: `populations`: every population is positive. dest[s, b * 16 + k] is the slot within slab group s that takes the k-th block of device b; every slot of a slab group appears once; dest[s, b * 16 + k] % 16 equals k; a device sends to any one owner, dest // 16, either none or exactly 1 of its blocks.
All inputs are finite; a program needn't handle non-finite values. No bound on the sum of `solid` or of `wetting` on one device may be relied on, other than what follows from the above.
Results may differ from the reference program's by a relative error of at most 0.0001.
Values sent between devices are 32-bit elements; how exact they have to be, the bound alone decides.
No kernel may reach another device: no remote copies, remote signals or barrier semaphores. Data moves between devices by JAX's collectives and lax.ppermute only.
A program may use at most 192 MiB of HBM per device.

```python
import math
import jax
import jax.numpy as jnp
import numpy as np
from jax import lax

B = 16
XB = 2
ZB = 8
NZ = 128
BPD = 16
NX = 128
NY = 512
N_SLAB = 4
N_BLK = 32


LATTICE_WEIGHTS = np.array([1.0 / 3.0] + [1.0 / 18.0] * 6 + [1.0 / 36.0] * 12)


def draw_populations(key, part):
    key = jax.random.fold_in(key, 5)
    grid_shape = (19, NX, NY, NZ)
    factor = jnp.exp(jax.random.uniform(key, grid_shape, jnp.float32, math.log(0.6), math.log(1.6)))
    weights = jnp.asarray(LATTICE_WEIGHTS, jnp.float32)
    return weights[:, None, None, None] * factor


def draw_dest(key, part):
    key = jax.random.fold_in(key, 11)
    spread_count = min(BPD, N_BLK)
    per_peer = BPD // spread_count

    def one_slab(slab_key):
        first_key, second_key = jax.random.split(slab_key)
        shuffle = jax.random.permutation(first_key, N_BLK).astype(jnp.int32)
        offsets = jax.random.permutation(second_key, N_BLK).astype(jnp.int32)[:spread_count]
        inverse = jnp.zeros((N_BLK,), jnp.int32).at[shuffle].set(jnp.arange(N_BLK, dtype=jnp.int32))
        device_index = jnp.arange(N_BLK, dtype=jnp.int32)[:, None]
        slot_index = jnp.arange(BPD, dtype=jnp.int32)[None, :]
        owner_device = inverse[(shuffle[device_index] + offsets[slot_index // per_peer]) % N_BLK]
        return (owner_device * BPD + slot_index).reshape(N_BLK * BPD)
    slab_keys = jax.random.split(key, N_SLAB)
    return jax.vmap(one_slab)(slab_keys).astype(jnp.int32)


def plant(result, stream_key, least, high):
    dims = result.shape
    place = [jax.random.randint(jax.random.fold_in(stream_key, axis), (), 0, dims[axis]) for axis in range(len(dims))]
    result = result.at[tuple(place)].set(least)
    longest = dims.index(max(dims))
    place[longest] = (place[longest] + 1) % dims[longest]
    return result.at[tuple(place)].set(high)


def setup_inputs(seed: int = 0) -> dict:
    seeds = jax.random.split(jax.random.key(seed), 5)
    populations = draw_populations(jax.random.fold_in(seeds[4], 71), 0)
    solid = plant((jax.random.randint(seeds[1], (NX, NY, NZ), 0, 5) < 2).astype(jnp.int32), jax.random.fold_in(seeds[1], 1), 0, 1)
    wetting = plant((jax.random.randint(seeds[2], (NX, NY, NZ), 0, 2) < 1).astype(jnp.int32), jax.random.fold_in(seeds[2], 1), 0, 1)
    dest = draw_dest(jax.random.fold_in(seeds[4], 71), 0)
    return dict(populations=populations, solid=solid, wetting=wetting, dest=dest)


VELOCITIES = np.array([[0, 0, 0], [1, 0, 0], [-1, 0, 0], [0, 1, 0], [0, -1, 0], [0, 0, 1], [0, 0, -1], [1, 1, 0], [-1, -1, 0], [1, -1, 0], [-1, 1, 0], [1, 0, 1], [-1, 0, -1], [1, 0, -1], [-1, 0, 1], [0, 1, 1], [0, -1, -1], [0, 1, -1], [0, -1, 1]])
OPPOSITE = [0, 2, 1, 4, 3, 6, 5, 8, 7, 10, 9, 12, 11, 14, 13, 16, 15, 18, 17]
LATTICE_WEIGHTS = np.array([1.0 / 3.0] + [1.0 / 18.0] * 6 + [1.0 / 36.0] * 12)
WALL_DENSITY = 1.2

def relaxation_table():
    along_x = VELOCITIES[:, 0] * 1.0
    along_y = VELOCITIES[:, 1] * 1.0
    along_z = VELOCITIES[:, 2] * 1.0
    unity = np.ones(19)
    monomials = [unity, along_x, along_y, along_z, along_x * along_x, along_y * along_y, along_z * along_z, along_x * along_y, along_y * along_z, along_x * along_z, along_x * along_y * along_y, along_x * along_z * along_z, along_y * along_x * along_x, along_y * along_z * along_z, along_z * along_x * along_x, along_z * along_y * along_y, along_x * along_x * along_y * along_y, along_y * along_y * along_z * along_z, along_z * along_z * along_x * along_x]
    basis = []
    for vector in monomials:
        residue = vector * 1.0
        for earlier in basis:
            residue = residue - np.dot(residue, earlier) * earlier
        basis.append(residue / np.sqrt(np.dot(residue, residue)))
    moments = np.stack(basis)
    rates = np.array([0.0] * 4 + [1.25] * 6 + [1.6] * 6 + [1.4] * 3)
    return np.dot(moments.T * rates[None, :], moments).astype(np.float32)

def collide(state):
    layout_shape = state.shape
    flattened = state.reshape(19, -1)
    velocity_rows = jnp.asarray(VELOCITIES.T, jnp.float32)
    velocity_cols = jnp.asarray(VELOCITIES, jnp.float32)
    density = lax.optimization_barrier(jnp.sum(flattened, axis=0))
    momentum = jnp.dot(velocity_rows, flattened, precision=lax.Precision.HIGHEST, preferred_element_type=jnp.float32)
    projected = jnp.dot(velocity_cols, momentum, precision=lax.Precision.HIGHEST, preferred_element_type=jnp.float32)
    squared = lax.optimization_barrier(jnp.sum(momentum * momentum, axis=0))
    weights = jnp.asarray(LATTICE_WEIGHTS, jnp.float32)[:, None]
    balance = weights * (density[None, :] + 3.0 * projected + 4.5 * projected * projected - 1.5 * squared[None, :])
    relaxed = flattened - jnp.dot(jnp.asarray(relaxation_table(), jnp.float32), flattened - balance, precision=lax.Precision.HIGHEST, preferred_element_type=jnp.float32)
    return relaxed.reshape(layout_shape)

def pull(padded, kind_padded, post):
    size_x = post.shape[1]
    size_y = post.shape[2]
    kind_here = kind_padded[1:-1, 1:-1]
    results = []
    for channel in range(19):
        step_x = int(VELOCITIES[channel, 0])
        step_y = int(VELOCITIES[channel, 1])
        step_z = int(VELOCITIES[channel, 2])
        source = padded[channel, 1 - step_x:1 - step_x + size_x, 1 - step_y:1 - step_y + size_y]
        source = jnp.roll(source, step_z, axis=-1)
        source_kind = kind_padded[1 - step_x:1 - step_x + size_x, 1 - step_y:1 - step_y + size_y]
        source_kind = jnp.roll(source_kind, step_z, axis=-1)
        reflected = post[OPPOSITE[channel]]
        wetted = 2.0 * WALL_DENSITY * float(LATTICE_WEIGHTS[channel]) - reflected
        pulled = jnp.where(source_kind == 1.0, source, jnp.where(source_kind == 2.0, wetted, reflected))
        results.append(jnp.where(kind_here == 1.0, pulled, 0.0))
    return jnp.stack(results)

def reference(populations, solid, wetting, dest):
    cell_kind = (1 - solid + 2 * solid * wetting).astype(jnp.float32)
    kind_padded = jnp.pad(cell_kind, ((1, 1), (1, 1), (0, 0)))
    pad_spec = ((0, 0), (1, 1), (1, 1), (0, 0))
    step_one = collide(pull(jnp.pad(populations, pad_spec), kind_padded, populations))
    read = pull(jnp.pad(step_one, pad_spec), kind_padded, step_one)
    collided = collide(read)
    blocks = collided.reshape(19, N_SLAB, XB, B, N_BLK, B, ZB, B)
    blocks = blocks.transpose(1, 4, 2, 6, 0, 3, 5, 7).reshape(N_SLAB, N_BLK * BPD, 19, B * B * B)
    slab_number = jnp.broadcast_to(jnp.arange(N_SLAB, dtype=jnp.int32)[:, None], dest.shape)
    placed = jnp.zeros_like(blocks).at[slab_number, dest.astype(jnp.int32)].set(blocks)
    return placed.reshape(N_SLAB * N_BLK * BPD, 19, B * B * B)
```

```python
import functools

import jax
import jax.numpy as jnp
import numpy as np
from jax import lax
from jax.experimental import pallas as pl
from jax.experimental.pallas import tpu as pltpu
from jax.sharding import PartitionSpec as P

VELOCITIES = [
    (0, 0, 0), (1, 0, 0), (-1, 0, 0), (0, 1, 0), (0, -1, 0), (0, 0, 1), (0, 0, -1),
    (1, 1, 0), (-1, -1, 0), (1, -1, 0), (-1, 1, 0), (1, 0, 1), (-1, 0, -1), (1, 0, -1),
    (-1, 0, 1), (0, 1, 1), (0, -1, -1), (0, 1, -1), (0, -1, 1),
]
OPPOSITE = [0, 2, 1, 4, 3, 6, 5, 8, 7, 10, 9, 12, 11, 14, 13, 16, 15, 18, 17]
WEIGHTS = [1.0 / 3.0] + [1.0 / 18.0] * 6 + [1.0 / 36.0] * 12
WALL_DENSITY = 1.2
BIG = 1e30
HALF_BIG = 1e29

X_UP = [i for i in range(19) if VELOCITIES[i][0] == 1]
X_DOWN = [i for i in range(19) if VELOCITIES[i][0] == -1]
Y_UP = [i for i in range(19) if VELOCITIES[i][1] == 1]
Y_DOWN = [i for i in range(19) if VELOCITIES[i][1] == -1]

XS, YS, ZS = 32, 16, 128
HALO_ROWS = 40
CHUNK = 4
CHUNKS = XS // CHUNK
BLOCKS = 16
BLOCK_ROWS = 19 * 32
PITCH = 33


def collide(f):
    s, d = {}, {}
    for i in range(1, 19, 2):
        s[i] = f[i] + f[i + 1]
        d[i] = f[i] - f[i + 1]
    sxy, sxz, syz = s[7] + s[9], s[11] + s[13], s[15] + s[17]
    sx, sy, sz = s[1], s[3], s[5]
    rho = f[0] + (sx + sy) + (sz + sxy) + (sxz + syz)
    jx = d[1] + (d[7] + d[9]) + (d[11] + d[13])
    jy = d[3] + (d[7] - d[9]) + (d[15] + d[17])
    jz = d[5] + (d[11] - d[13]) + (d[15] - d[17])
    xx, yy, zz = jx * jx, jy * jy, jz * jz
    r = rho - 1.5 * (xx + yy + zz)
    tx, ty, tz = 2.0 * sx + 0.5 * xx, 2.0 * sy + 0.5 * yy, 2.0 * sz + 0.5 * zz
    base = 4.0 * f[0] - r
    qxy = (sxy - tx) + (base - ty + (xx + yy))
    qyz = (syz - ty) + (base - tz + (yy + zz))
    qxz = (sxz - tx) + (base - tz + (xx + zz))
    mean = (qxy + qyz + qxz) * (2.0 / 7.0)
    scale = 0.15 / 12.0
    a, b, c = (qxy - mean) * scale, (qyz - mean) * scale, (qxz - mean) * scale
    out = [None] * 19
    out[0] = -0.25 * f[0] + (1.25 / 3.0) * r - 4.0 * (a + b + c)
    axis_r = (1.25 / 18.0) * r
    plane_r = (1.25 / 36.0) * r

    def pair(i, along, square, even):
        w = WEIGHTS[i]
        e = even - 0.125 * s[i] + (1.25 * 4.5 * w) * square
        o = (1.6 * 3.0 * w) * along - 0.3 * d[i]
        out[i] = e + o
        out[i + 1] = e - o

    pair(1, jx, xx, axis_r + 2.0 * (a + c))
    pair(3, jy, yy, axis_r + 2.0 * (a + b))
    pair(5, jz, zz, axis_r + 2.0 * (b + c))
    for i, u, even in ((7, jx + jy, plane_r - a), (9, jx - jy, plane_r - a), (11, jx + jz, plane_r - c),
                       (13, jx - jz, plane_r - c), (15, jy + jz, plane_r - b), (17, jy - jz, plane_r - b)):
        pair(i, u, u * u, even)
    return out


def pull(own, source, y_row):
    row = lax.broadcasted_iota(jnp.int32, (YS, ZS), 0)
    mine = [own(i) for i in range(19)]
    out = [mine[0]]
    for i in range(1, 19):
        cx, cy, cz = VELOCITIES[i]
        v = source(i)
        if cy == 1:
            v = jnp.where(row == 0, y_row(i), pltpu.roll(v, 1, 0))
        elif cy == -1:
            v = jnp.where(row == YS - 1, y_row(i), pltpu.roll(v, YS - 1, 0))
        if cz:
            v = pltpu.roll(v, cz % ZS, 1)
        reflected = mine[OPPOSITE[i]]
        wall = jnp.where(v > 0.0, reflected, 2.0 * WALL_DENSITY * WEIGHTS[i] - reflected)
        out.append(jnp.where(jnp.abs(v) < HALF_BIG, v, wall))
    return out


def fetch(hbm, vmem, sem):
    return [
        pltpu.make_async_copy(
            hbm.at[:, pl.ds(c * CHUNK, CHUNK)], vmem.at[:, pl.ds(1 + c * CHUNK, CHUNK)], sem.at[c]
        )
        for c in range(CHUNKS)
    ]


def place_x_halo(f, xlo, xhi):
    first = lax.axis_index("slab") == 0
    last = lax.axis_index("slab") == lax.axis_size("slab") - 1
    for k in range(5):
        f[X_UP[k], 0] = jnp.where(first, BIG, xlo[k])
        f[X_DOWN[k], XS + 1] = jnp.where(last, BIG, xhi[k])


def y_rows(ylo, yhi, x):
    first = lax.axis_index("blk") == 0
    last = lax.axis_index("blk") == lax.axis_size("blk") - 1

    def y_row(i):
        at = x + 1 - VELOCITIES[i][0]
        if i in Y_UP:
            return jnp.where(first, BIG, ylo[Y_UP.index(i), pl.ds(at, 1), :])
        return jnp.where(last, BIG, yhi[Y_DOWN.index(i), pl.ds(at, 1), :])

    return y_row


def step_one_kernel(pops, solid, wetting, xlo, xhi, ylo, yhi, out, xup, xdn, yup, ydn, f, mark, res, sem_in, sem_out):
    copies = fetch(pops, f, sem_in)
    for copy in copies:
        copy.start()
    place_x_halo(f, xlo, xhi)
    mark[0] = jnp.zeros((YS, ZS), jnp.float32)
    mark[XS + 1] = jnp.zeros((YS, ZS), jnp.float32)

    def marks(x, carry):
        mark[x + 1] = jnp.where(solid[x] == 1, jnp.where(wetting[x] == 1, -BIG, BIG), 0.0)
        return carry

    lax.fori_loop(0, XS, marks, 0)

    def plane(x, carry):
        marked = {c: mark[x + 1 - c] for c in (-1, 0, 1)}

        def source(i):
            c = VELOCITIES[i][0]
            return jnp.where(marked[c] == 0.0, f[i, x + 1 - c], marked[c])

        pulled = pull(lambda i: f[i, x + 1], source, y_rows(ylo, yhi, x))
        new = collide(pulled)
        here = marked[0]
        for i in range(19):
            value = jnp.where(here == 0.0, new[i], here)
            res[i, x] = value
            if i in Y_UP:
                yup[Y_UP.index(i), pl.ds(x + 1, 1), :] = value[YS - 1 : YS]
            if i in Y_DOWN:
                ydn[Y_DOWN.index(i), pl.ds(x + 1, 1), :] = value[0:1]
        return carry

    outs = []
    copies[0].wait()
    for c in range(CHUNKS):
        if c + 1 < CHUNKS:
            copies[c + 1].wait()
        lax.fori_loop(c * CHUNK, (c + 1) * CHUNK, plane, 0)
        at = pl.ds(c * CHUNK, CHUNK)
        outs.append(pltpu.make_async_copy(res.at[:, at], out.at[:, at], sem_out.at[c]))
        outs[-1].start()
    for k in range(5):
        xup[k] = res[X_UP[k], XS - 1]
        xdn[k] = res[X_DOWN[k], 0]
    for copy in outs:
        copy.wait()


def step_two_kernel(owners, f1, xlo, xhi, ylo, yhi, outgoing, f, col, buf, sem_in, sem_out):
    copies = fetch(f1, f, sem_in)
    for copy in copies:
        copy.start()
    place_x_halo(f, xlo, xhi)
    lane_block = lax.broadcasted_iota(jnp.int32, (8, ZS), 1) // 16

    def group(c):
        def plane(k, carry):
            x = c * CHUNK + k
            new = collide(
                pull(
                    lambda i: f[i, x + 1],
                    lambda i: f[i, x + 1 - VELOCITIES[i][0]],
                    y_rows(ylo, yhi, x),
                )
            )
            fluid = jnp.abs(f[0, x + 1]) < HALF_BIG
            for i in range(19):
                col[i, k] = jnp.where(fluid, new[i], 0.0)
            return carry

        lax.fori_loop(0, CHUNK, plane, 0)
        first = (c // 4) * 8

        def channel(i, carry):
            v = [col[i, r // 2, (r % 2) * 8 : (r % 2) * 8 + 8, :] for r in range(8)]
            for w in (4, 2, 1):
                high = (lane_block & w) != 0
                for r in range(8):
                    if r & w == 0:
                        a, b = v[r], v[r | w]
                        v[r] = jnp.where(high, pltpu.roll(b, 16 * w, 1), a)
                        v[r | w] = jnp.where(high, b, pltpu.roll(a, ZS - 16 * w, 1))
            at = pl.multiple_of(i * 32 + (c % 4) * 8, 8)
            for r in range(8):
                buf[first + r, pl.ds(at, 8), :] = v[r]
            return carry

        lax.fori_loop(0, 19, channel, 0)

    outs = []
    copies[0].wait()
    for c in range(CHUNKS):
        if c + 1 < CHUNKS:
            copies[c + 1].wait()
        group(c)
        if c % 4 == 3:
            for k in range((c // 4) * 8, (c // 4) * 8 + 8):
                outs.append(pltpu.make_async_copy(buf.at[k], outgoing.at[owners[k]], sem_out.at[k]))
                outs[-1].start()
    for copy in outs:
        copy.wait()


def place_kernel(sources, incoming, out, rows):
    del sources
    sub = lax.broadcasted_iota(jnp.int32, (8, ZS), 0)
    lane_block = lax.broadcasted_iota(jnp.int32, (8, ZS), 1) // 16
    pick = (lane_block + sub + 1) & 7
    for i in range(19):
        for q in range(4):
            v = incoming[0, i * 32 + q * 8 : i * 32 + q * 8 + 8, :]
            v = pltpu.roll(v, 0, 1, stride=16, stride_axis=0)
            v = jnp.take_along_axis(v, pick, axis=0)
            v = pltpu.roll(v, 16, 1, stride=16, stride_axis=0)
            rows[pl.ds(i * PITCH + q * 8, 8), :] = v
    for j in range(32):
        out[0, :, j * 128 : (j + 1) * 128] = rows[pl.ds(j // 8 * 8 + 7 - j % 8, 19, stride=PITCH), :]


VMEM = pl.BlockSpec(memory_space=pltpu.VMEM)
ANY = pl.BlockSpec(memory_space=pl.ANY)
SMEM = pl.BlockSpec(memory_space=pltpu.SMEM)


def sds(*shape):
    return jax.ShapeDtypeStruct(shape, jnp.float32)


def params():
    return pltpu.CompilerParams(vmem_limit_bytes=48 * 1024 * 1024)


def step_one(pops, solid, wetting, halo):
    return pl.pallas_call(
        step_one_kernel,
        out_shape=(sds(19, XS, YS, ZS), sds(5, YS, ZS), sds(5, YS, ZS), sds(5, HALO_ROWS, ZS), sds(5, HALO_ROWS, ZS)),
        in_specs=[ANY] + [VMEM] * 6,
        out_specs=(ANY, VMEM, VMEM, VMEM, VMEM),
        scratch_shapes=[
            pltpu.VMEM((19, XS + 2, YS, ZS), jnp.float32),
            pltpu.VMEM((XS + 2, YS, ZS), jnp.float32),
            pltpu.VMEM((19, XS, YS, ZS), jnp.float32),
            pltpu.SemaphoreType.DMA((CHUNKS,)),
            pltpu.SemaphoreType.DMA((CHUNKS,)),
        ],
        compiler_params=params(),
        name="step_one",
    )(pops, solid, wetting, *halo)


def step_two(owners, f1, halo, peers):
    return pl.pallas_call(
        step_two_kernel,
        out_shape=sds(peers, BLOCK_ROWS, ZS),
        in_specs=[SMEM, ANY] + [VMEM] * 4,
        out_specs=ANY,
        scratch_shapes=[
            pltpu.VMEM((19, XS + 2, YS, ZS), jnp.float32),
            pltpu.VMEM((19, CHUNK, YS, ZS), jnp.float32),
            pltpu.VMEM((BLOCKS, BLOCK_ROWS, ZS), jnp.float32),
            pltpu.SemaphoreType.DMA((CHUNKS,)),
            pltpu.SemaphoreType.DMA((BLOCKS,)),
        ],
        compiler_params=params(),
        name="step_two",
    )(owners, f1, *halo)


def place(sources, incoming):
    return pl.pallas_call(
        place_kernel,
        out_shape=sds(BLOCKS, 19, 4096),
        grid_spec=pltpu.PrefetchScalarGridSpec(
            num_scalar_prefetch=1,
            grid=(BLOCKS,),
            in_specs=[pl.BlockSpec((1, BLOCK_ROWS, ZS), lambda j, src: (src[j], 0, 0))],
            out_specs=pl.BlockSpec((1, 19, 4096), lambda j, src: (j, 0, 0)),
            scratch_shapes=[pltpu.VMEM((640, ZS), jnp.float32)],
        ),
        compiler_params=params(),
        name="place",
    )(sources, incoming)


def shift(value, axis, up):
    count = lax.axis_size(axis)
    steps = [(i, i + 1) if up else (i + 1, i) for i in range(count - 1)]
    return lax.ppermute(value, axis, steps)


def exchange(xup, xdn, yup, ydn):
    xlo, xhi = shift(xup, "slab", True), shift(xdn, "slab", False)
    first = lax.axis_index("slab") == 0
    last = lax.axis_index("slab") == lax.axis_size("slab") - 1
    row = jnp.arange(HALO_ROWS)[:, None]

    def corners(rows, lo_channel, hi_channel, y, channels):
        parts = []
        for k, i in enumerate(channels):
            part = rows[k]
            if i == lo_channel:
                part = jnp.where(row == 0, jnp.where(first, BIG, xlo[X_UP.index(i), y]), part)
            if i == hi_channel:
                part = jnp.where(row == XS + 1, jnp.where(last, BIG, xhi[X_DOWN.index(i), y]), part)
            parts.append(part)
        return jnp.stack(parts)

    yup = corners(yup, 7, 10, YS - 1, Y_UP)
    ydn = corners(ydn, 9, 8, 0, Y_DOWN)
    return xlo, xhi, shift(yup, "blk", True), shift(ydn, "blk", False)


def per_device(populations, solid, wetting, dest):
    me = lax.axis_index("blk")
    peers = lax.axis_size("blk")
    everyone = lax.all_gather(dest[0], "blk")
    mark = jnp.where(solid == 1, jnp.where(wetting == 1, -BIG, BIG), 0.0)

    def marked(channels, x, y):
        m = mark[x, y]
        return jnp.where(m == 0.0, jnp.stack([populations[i, x, y] for i in channels]), m)

    every = slice(None)
    grow = ((0, 0), (1, HALO_ROWS - XS - 1), (0, 0))
    halo = exchange(
        marked(X_UP, XS - 1, every),
        marked(X_DOWN, 0, every),
        jnp.pad(marked(Y_UP, every, YS - 1), grow),
        jnp.pad(marked(Y_DOWN, every, 0), grow),
    )
    f1, *edges = step_one(populations, solid, wetting, halo)
    outgoing = step_two(dest[0] // BLOCKS, f1, exchange(*edges), peers)
    incoming = lax.all_to_all(outgoing, "blk", split_axis=0, concat_axis=0, tiled=True)
    mine = everyone // BLOCKS == me
    sources = jnp.sum(jnp.where(mine, jnp.arange(peers, dtype=jnp.int32)[:, None], 0), axis=0)
    return place(sources, incoming)


def solution(mesh):
    in_specs = (
        P(None, "slab", "blk", None),
        P("slab", "blk", None),
        P("slab", "blk", None),
        P("slab", "blk"),
    )
    out_specs = P(("slab", "blk"), None, None)
    return jax.shard_map(
        per_device, mesh=mesh, in_specs=in_specs, out_specs=out_specs, check_vma=False
    )
```

```python
import functools

import jax
import jax.numpy as jnp
import numpy as np
from jax import lax
from jax.experimental import pallas as pl
from jax.experimental.pallas import tpu as pltpu
from jax.sharding import PartitionSpec as P

VELOCITIES = [
    (0, 0, 0), (1, 0, 0), (-1, 0, 0), (0, 1, 0), (0, -1, 0), (0, 0, 1), (0, 0, -1),
    (1, 1, 0), (-1, -1, 0), (1, -1, 0), (-1, 1, 0), (1, 0, 1), (-1, 0, -1), (1, 0, -1),
    (-1, 0, 1), (0, 1, 1), (0, -1, -1), (0, 1, -1), (0, -1, 1),
]
OPPOSITE = [0, 2, 1, 4, 3, 6, 5, 8, 7, 10, 9, 12, 11, 14, 13, 16, 15, 18, 17]
WEIGHTS = [1.0 / 3.0] + [1.0 / 18.0] * 6 + [1.0 / 36.0] * 12
WALL_DENSITY = 1.2
BIG = 1e30
HALF_BIG = 1e29

X_UP = [i for i in range(19) if VELOCITIES[i][0] == 1]
X_DOWN = [i for i in range(19) if VELOCITIES[i][0] == -1]
Y_UP = [i for i in range(19) if VELOCITIES[i][1] == 1]
Y_DOWN = [i for i in range(19) if VELOCITIES[i][1] == -1]

XS, YS, ZS = 32, 16, 128
HALO_ROWS = 40
CHUNK = 4
CHUNKS = XS // CHUNK
BLOCKS = 16
BLOCK_ROWS = 19 * 32
SLOT_ROWS = BLOCK_ROWS + 8


def collide(f):
    s, d = {}, {}
    for i in range(1, 19, 2):
        s[i] = f[i] + f[i + 1]
        d[i] = f[i] - f[i + 1]
    sxy, sxz, syz = s[7] + s[9], s[11] + s[13], s[15] + s[17]
    sx, sy, sz = s[1], s[3], s[5]
    rho = f[0] + (sx + sy) + (sz + sxy) + (sxz + syz)
    jx = d[1] + (d[7] + d[9]) + (d[11] + d[13])
    jy = d[3] + (d[7] - d[9]) + (d[15] + d[17])
    jz = d[5] + (d[11] - d[13]) + (d[15] - d[17])
    xx, yy, zz = jx * jx, jy * jy, jz * jz
    r = rho - 1.5 * (xx + yy + zz)
    tx, ty, tz = 2.0 * sx + 0.5 * xx, 2.0 * sy + 0.5 * yy, 2.0 * sz + 0.5 * zz
    base = 4.0 * f[0] - r
    qxy = (sxy - tx) + (base - ty + (xx + yy))
    qyz = (syz - ty) + (base - tz + (yy + zz))
    qxz = (sxz - tx) + (base - tz + (xx + zz))
    mean = (qxy + qyz + qxz) * (2.0 / 7.0)
    scale = 0.15 / 12.0
    a, b, c = (qxy - mean) * scale, (qyz - mean) * scale, (qxz - mean) * scale
    out = [None] * 19
    out[0] = -0.25 * f[0] + (1.25 / 3.0) * r - 4.0 * (a + b + c)
    axis_r = (1.25 / 18.0) * r
    plane_r = (1.25 / 36.0) * r

    def pair(i, along, square, even):
        w = WEIGHTS[i]
        e = even - 0.125 * s[i] + (1.25 * 4.5 * w) * square
        o = (1.6 * 3.0 * w) * along - 0.3 * d[i]
        out[i] = e + o
        out[i + 1] = e - o

    pair(1, jx, xx, axis_r + 2.0 * (a + c))
    pair(3, jy, yy, axis_r + 2.0 * (a + b))
    pair(5, jz, zz, axis_r + 2.0 * (b + c))
    for i, u, even in ((7, jx + jy, plane_r - a), (9, jx - jy, plane_r - a), (11, jx + jz, plane_r - c),
                       (13, jx - jz, plane_r - c), (15, jy + jz, plane_r - b), (17, jy - jz, plane_r - b)):
        pair(i, u, u * u, even)
    return out


def pull(own, source, y_row):
    row = lax.broadcasted_iota(jnp.int32, (YS, ZS), 0)
    mine = [own(i) for i in range(19)]
    out = [mine[0]]
    for i in range(1, 19):
        cx, cy, cz = VELOCITIES[i]
        v = source(i)
        if cy == 1:
            v = jnp.where(row == 0, y_row(i), pltpu.roll(v, 1, 0))
        elif cy == -1:
            v = jnp.where(row == YS - 1, y_row(i), pltpu.roll(v, YS - 1, 0))
        if cz:
            v = pltpu.roll(v, cz % ZS, 1)
        reflected = mine[OPPOSITE[i]]
        wall = jnp.where(v > 0.0, reflected, 2.0 * WALL_DENSITY * WEIGHTS[i] - reflected)
        out.append(jnp.where(jnp.abs(v) < HALF_BIG, v, wall))
    return out


def fetch(hbm, vmem, sem):
    return [
        pltpu.make_async_copy(
            hbm.at[:, pl.ds(c * CHUNK, CHUNK)], vmem.at[:, pl.ds(1 + c * CHUNK, CHUNK)], sem.at[c]
        )
        for c in range(CHUNKS)
    ]


def place_x_halo(f, xlo, xhi):
    first = lax.axis_index("slab") == 0
    last = lax.axis_index("slab") == lax.axis_size("slab") - 1
    for k in range(5):
        f[X_UP[k], 0] = jnp.where(first, BIG, xlo[k])
        f[X_DOWN[k], XS + 1] = jnp.where(last, BIG, xhi[k])


def y_rows(ylo, yhi, x):
    first = lax.axis_index("blk") == 0
    last = lax.axis_index("blk") == lax.axis_size("blk") - 1

    def y_row(i):
        at = x + 1 - VELOCITIES[i][0]
        if i in Y_UP:
            return jnp.where(first, BIG, ylo[Y_UP.index(i), pl.ds(at, 1), :])
        return jnp.where(last, BIG, yhi[Y_DOWN.index(i), pl.ds(at, 1), :])

    return y_row


def step_one_kernel(pops, solid, wetting, xlo, xhi, ylo, yhi, out, xup, xdn, yup, ydn, f, mark, res, sem_in, sem_out):
    copies = fetch(pops, f, sem_in)
    for copy in copies:
        copy.start()
    place_x_halo(f, xlo, xhi)
    mark[0] = jnp.zeros((YS, ZS), jnp.float32)
    mark[XS + 1] = jnp.zeros((YS, ZS), jnp.float32)

    def marks(x, carry):
        mark[x + 1] = jnp.where(solid[x] == 1, jnp.where(wetting[x] == 1, -BIG, BIG), 0.0)
        return carry

    lax.fori_loop(0, XS, marks, 0)

    def plane(x, carry):
        marked = {c: mark[x + 1 - c] for c in (-1, 0, 1)}

        def source(i):
            c = VELOCITIES[i][0]
            return jnp.where(marked[c] == 0.0, f[i, x + 1 - c], marked[c])

        pulled = pull(lambda i: f[i, x + 1], source, y_rows(ylo, yhi, x))
        new = collide(pulled)
        here = marked[0]
        for i in range(19):
            value = jnp.where(here == 0.0, new[i], here)
            res[i, x] = value
            if i in Y_UP:
                yup[Y_UP.index(i), pl.ds(x + 1, 1), :] = value[YS - 1 : YS]
            if i in Y_DOWN:
                ydn[Y_DOWN.index(i), pl.ds(x + 1, 1), :] = value[0:1]
        return carry

    outs = []
    copies[0].wait()
    for c in range(CHUNKS):
        if c + 1 < CHUNKS:
            copies[c + 1].wait()
        lax.fori_loop(c * CHUNK, (c + 1) * CHUNK, plane, 0)
        at = pl.ds(c * CHUNK, CHUNK)
        outs.append(pltpu.make_async_copy(res.at[:, at], out.at[:, at], sem_out.at[c]))
        outs[-1].start()
    for k in range(5):
        xup[k] = res[X_UP[k], XS - 1]
        xdn[k] = res[X_DOWN[k], 0]
    for copy in outs:
        copy.wait()


def step_two_kernel(owners, f1, xlo, xhi, ylo, yhi, outgoing, f, buf, absent, sem_in, sem_absent, sem_out):
    copies = fetch(f1, f, sem_in)
    for copy in copies:
        copy.start()
    absent[...] = jnp.full((8, ZS), -1.0, jnp.float32)
    label_rows = pl.ds(BLOCK_ROWS, 8)
    clears = [
        pltpu.make_async_copy(absent, outgoing.at[p, label_rows], sem_absent.at[p])
        for p in range(outgoing.shape[0])
    ]
    for clear in clears:
        clear.start()
    for k in range(BLOCKS):
        at = (k // 8 * 8 + 7 - k % 8) * SLOT_ROWS + BLOCK_ROWS
        buf[at : at + 8, :] = jnp.full((8, ZS), float(k), jnp.float32)
    place_x_halo(f, xlo, xhi)
    sub = lax.broadcasted_iota(jnp.int32, (8, ZS), 0)
    lane_block = lax.broadcasted_iota(jnp.int32, (8, ZS), 1) // 16
    pick = (lane_block + sub + 1) & 7

    def plane(x, carry):
        new = collide(
            pull(
                lambda i: f[i, x + 1],
                lambda i: f[i, x + 1 - VELOCITIES[i][0]],
                y_rows(ylo, yhi, x),
            )
        )
        fluid = jnp.abs(f[0, x + 1]) < HALF_BIG
        base = x // 16 * (8 * SLOT_ROWS) + x % 16 * 2
        for i in range(19):
            value = jnp.where(fluid, new[i], 0.0)
            for half in range(2):
                v = pltpu.roll(value[half * 8 : half * 8 + 8], 0, 1, stride=16, stride_axis=0)
                v = jnp.take_along_axis(v, pick, axis=0)
                v = pltpu.roll(v, 16, 1, stride=16, stride_axis=0)
                buf[pl.ds(base + i * 32 + half, 8, stride=SLOT_ROWS + 1), :] = v
        return carry

    outs = []
    copies[0].wait()
    for c in range(CHUNKS):
        if c + 1 < CHUNKS:
            copies[c + 1].wait()
        lax.fori_loop(c * CHUNK, (c + 1) * CHUNK, plane, 0)
        if c == 0:
            for clear in clears:
                clear.wait()
        if c % 4 == 3:
            for k in range(c // 4 * 8, c // 4 * 8 + 8):
                at = (k // 8 * 8 + 7 - k % 8) * SLOT_ROWS
                outs.append(
                    pltpu.make_async_copy(
                        buf.at[pl.ds(at, SLOT_ROWS)], outgoing.at[owners[k]], sem_out.at[k]
                    )
                )
                outs[-1].start()
    for copy in outs:
        copy.wait()


def place_kernel(incoming, out, labels, blocks, res, sem_label, sem_in, sem_out):
    peers = incoming.shape[0]
    copy = pltpu.make_async_copy(incoming.at[:, pl.ds(BLOCK_ROWS, 8)], labels, sem_label)
    copy.start()
    copy.wait()
    lane = lax.broadcasted_iota(jnp.int32, (1, ZS), 1)
    slot = lane.astype(jnp.float32)
    found = jnp.zeros((1, ZS), jnp.int32)
    for p in range(peers):
        found += jnp.where(labels[p, 7:8, :] == slot, p, 0)
    ins = []
    for k in range(BLOCKS):
        source = jnp.clip(jnp.sum(jnp.where(lane == k, found, 0)), 0, peers - 1)
        ins.append(
            pltpu.make_async_copy(
                incoming.at[source], blocks.at[pl.ds(k * SLOT_ROWS, SLOT_ROWS)], sem_in.at[k]
            )
        )
        ins[-1].start()
    outs = []
    for h in range(2):
        for k in range(8):
            ins[h * 8 + k].wait()

        def channel(i, carry):
            for j in range(32):
                at = h * 8 * SLOT_ROWS + 7 + i * 32 + j
                res[i, h * 8 : h * 8 + 8, j * 128 : (j + 1) * 128] = blocks[
                    pl.ds(at, 8, stride=SLOT_ROWS - 1), :
                ]
            return carry

        for part, (low, high) in enumerate(((0, 5), (5, 10), (10, 15), (15, 19))):
            lax.fori_loop(low, high, channel, 0)
            at = (pl.ds(low, high - low), pl.ds(h * 8, 8))
            outs.append(pltpu.make_async_copy(res.at[at], out.at[at], sem_out.at[h * 4 + part]))
            outs[-1].start()
    for copy in outs:
        copy.wait()


VMEM = pl.BlockSpec(memory_space=pltpu.VMEM)
ANY = pl.BlockSpec(memory_space=pl.ANY)
SMEM = pl.BlockSpec(memory_space=pltpu.SMEM)


def sds(*shape):
    return jax.ShapeDtypeStruct(shape, jnp.float32)


def params():
    return pltpu.CompilerParams(vmem_limit_bytes=48 * 1024 * 1024)


def step_one(pops, solid, wetting, halo):
    return pl.pallas_call(
        step_one_kernel,
        out_shape=(sds(19, XS, YS, ZS), sds(5, YS, ZS), sds(5, YS, ZS), sds(5, HALO_ROWS, ZS), sds(5, HALO_ROWS, ZS)),
        in_specs=[ANY] + [VMEM] * 6,
        out_specs=(ANY, VMEM, VMEM, VMEM, VMEM),
        scratch_shapes=[
            pltpu.VMEM((19, XS + 2, YS, ZS), jnp.float32),
            pltpu.VMEM((XS + 2, YS, ZS), jnp.float32),
            pltpu.VMEM((19, XS, YS, ZS), jnp.float32),
            pltpu.SemaphoreType.DMA((CHUNKS,)),
            pltpu.SemaphoreType.DMA((CHUNKS,)),
        ],
        compiler_params=params(),
        name="step_one",
    )(pops, solid, wetting, *halo)


def step_two(owners, f1, halo, peers):
    return pl.pallas_call(
        step_two_kernel,
        out_shape=sds(peers, SLOT_ROWS, ZS),
        in_specs=[SMEM, ANY] + [VMEM] * 4,
        out_specs=ANY,
        scratch_shapes=[
            pltpu.VMEM((19, XS + 2, YS, ZS), jnp.float32),
            pltpu.VMEM((BLOCKS * SLOT_ROWS, ZS), jnp.float32),
            pltpu.VMEM((8, ZS), jnp.float32),
            pltpu.SemaphoreType.DMA((CHUNKS,)),
            pltpu.SemaphoreType.DMA((peers,)),
            pltpu.SemaphoreType.DMA((BLOCKS,)),
        ],
        compiler_params=params(),
        name="step_two",
    )(owners, f1, *halo)


def place(incoming):
    peers = incoming.shape[0]
    return pl.pallas_call(
        place_kernel,
        out_shape=sds(19, BLOCKS, 4096),
        in_specs=[ANY],
        out_specs=ANY,
        scratch_shapes=[
            pltpu.VMEM((peers, 8, ZS), jnp.float32),
            pltpu.VMEM((BLOCKS * SLOT_ROWS, ZS), jnp.float32),
            pltpu.VMEM((19, BLOCKS, 4096), jnp.float32),
            pltpu.SemaphoreType.DMA,
            pltpu.SemaphoreType.DMA((BLOCKS,)),
            pltpu.SemaphoreType.DMA((8,)),
        ],
        compiler_params=params(),
        name="place",
    )(incoming)


def shift(value, axis, up):
    count = lax.axis_size(axis)
    steps = [(i, i + 1) if up else (i + 1, i) for i in range(count - 1)]
    return lax.ppermute(value, axis, steps)


def exchange(xup, xdn, yup, ydn):
    xlo, xhi = shift(xup, "slab", True), shift(xdn, "slab", False)
    first = lax.axis_index("slab") == 0
    last = lax.axis_index("slab") == lax.axis_size("slab") - 1
    row = jnp.arange(HALO_ROWS)[:, None]

    def corners(rows, lo_channel, hi_channel, y, channels):
        parts = []
        for k, i in enumerate(channels):
            part = rows[k]
            if i == lo_channel:
                part = jnp.where(row == 0, jnp.where(first, BIG, xlo[X_UP.index(i), y]), part)
            if i == hi_channel:
                part = jnp.where(row == XS + 1, jnp.where(last, BIG, xhi[X_DOWN.index(i), y]), part)
            parts.append(part)
        return jnp.stack(parts)

    yup = corners(yup, 7, 10, YS - 1, Y_UP)
    ydn = corners(ydn, 9, 8, 0, Y_DOWN)
    return xlo, xhi, shift(yup, "blk", True), shift(ydn, "blk", False)


def per_device(populations, solid, wetting, dest):
    peers = lax.axis_size("blk")
    mark = jnp.where(solid == 1, jnp.where(wetting == 1, -BIG, BIG), 0.0)

    def marked(channels, x, y):
        m = mark[x, y]
        return jnp.where(m == 0.0, jnp.stack([populations[i, x, y] for i in channels]), m)

    every = slice(None)
    grow = ((0, 0), (1, HALO_ROWS - XS - 1), (0, 0))
    halo = exchange(
        marked(X_UP, XS - 1, every),
        marked(X_DOWN, 0, every),
        jnp.pad(marked(Y_UP, every, YS - 1), grow),
        jnp.pad(marked(Y_DOWN, every, 0), grow),
    )
    f1, *edges = step_one(populations, solid, wetting, halo)
    outgoing = step_two(dest[0] // BLOCKS, f1, exchange(*edges), peers)
    incoming = lax.all_to_all(outgoing, "blk", split_axis=0, concat_axis=0, tiled=True)
    return place(incoming).transpose(1, 0, 2)


def solution(mesh):
    in_specs = (
        P(None, "slab", "blk", None),
        P("slab", "blk", None),
        P("slab", "blk", None),
        P("slab", "blk"),
    )
    out_specs = P(("slab", "blk"), None, None)
    return jax.shard_map(
        per_device, mesh=mesh, in_specs=in_specs, out_specs=out_specs, check_vma=False
    )
```

```python
import functools

import jax
import jax.numpy as jnp
import numpy as np
from jax import lax
from jax.experimental import pallas as pl
from jax.experimental.pallas import tpu as pltpu
from jax.sharding import PartitionSpec as P

VELOCITIES = [
    (0, 0, 0), (1, 0, 0), (-1, 0, 0), (0, 1, 0), (0, -1, 0), (0, 0, 1), (0, 0, -1),
    (1, 1, 0), (-1, -1, 0), (1, -1, 0), (-1, 1, 0), (1, 0, 1), (-1, 0, -1), (1, 0, -1),
    (-1, 0, 1), (0, 1, 1), (0, -1, -1), (0, 1, -1), (0, -1, 1),
]
OPPOSITE = [0, 2, 1, 4, 3, 6, 5, 8, 7, 10, 9, 12, 11, 14, 13, 16, 15, 18, 17]
WEIGHTS = [1.0 / 3.0] + [1.0 / 18.0] * 6 + [1.0 / 36.0] * 12
WALL_DENSITY = 1.2
BIG = 1e30
HALF_BIG = 1e29

X_UP = [i for i in range(19) if VELOCITIES[i][0] == 1]
X_DOWN = [i for i in range(19) if VELOCITIES[i][0] == -1]
Y_UP = [i for i in range(19) if VELOCITIES[i][1] == 1]
Y_DOWN = [i for i in range(19) if VELOCITIES[i][1] == -1]

XS, YS, ZS = 32, 16, 128
HALO_ROWS = 40
CHUNK = 4
CHUNKS = XS // CHUNK
BLOCKS = 16
BLOCK_ROWS = 19 * 32
SLOT_ROWS = BLOCK_ROWS + 8


def collide(f):
    s, d = {}, {}
    for i in range(1, 19, 2):
        s[i] = f[i] + f[i + 1]
        d[i] = f[i] - f[i + 1]
    sxy, sxz, syz = s[7] + s[9], s[11] + s[13], s[15] + s[17]
    sx, sy, sz = s[1], s[3], s[5]
    rho = f[0] + (sx + sy) + (sz + sxy) + (sxz + syz)
    jx = d[1] + (d[7] + d[9]) + (d[11] + d[13])
    jy = d[3] + (d[7] - d[9]) + (d[15] + d[17])
    jz = d[5] + (d[11] - d[13]) + (d[15] - d[17])
    xx, yy, zz = jx * jx, jy * jy, jz * jz
    r = rho - 1.5 * (xx + yy + zz)
    tx, ty, tz = 2.0 * sx + 0.5 * xx, 2.0 * sy + 0.5 * yy, 2.0 * sz + 0.5 * zz
    base = 4.0 * f[0] - r
    qxy = (sxy - tx) + (base - ty + (xx + yy))
    qyz = (syz - ty) + (base - tz + (yy + zz))
    qxz = (sxz - tx) + (base - tz + (xx + zz))
    mean = (qxy + qyz + qxz) * (2.0 / 7.0)
    scale = 0.15 / 12.0
    a, b, c = (qxy - mean) * scale, (qyz - mean) * scale, (qxz - mean) * scale
    out = [None] * 19
    out[0] = -0.25 * f[0] + (1.25 / 3.0) * r - 4.0 * (a + b + c)
    axis_r = (1.25 / 18.0) * r
    plane_r = (1.25 / 36.0) * r

    def pair(i, along, square, even):
        w = WEIGHTS[i]
        e = even - 0.125 * s[i] + (1.25 * 4.5 * w) * square
        o = (1.6 * 3.0 * w) * along - 0.3 * d[i]
        out[i] = e + o
        out[i + 1] = e - o

    pair(1, jx, xx, axis_r + 2.0 * (a + c))
    pair(3, jy, yy, axis_r + 2.0 * (a + b))
    pair(5, jz, zz, axis_r + 2.0 * (b + c))
    for i, u, even in ((7, jx + jy, plane_r - a), (9, jx - jy, plane_r - a), (11, jx + jz, plane_r - c),
                       (13, jx - jz, plane_r - c), (15, jy + jz, plane_r - b), (17, jy - jz, plane_r - b)):
        pair(i, u, u * u, even)
    return out


def pull(own, source, y_row):
    row = lax.broadcasted_iota(jnp.int32, (YS, ZS), 0)
    mine = [own(i) for i in range(19)]
    out = [mine[0]]
    for i in range(1, 19):
        cx, cy, cz = VELOCITIES[i]
        v = source(i)
        if cy == 1:
            v = jnp.where(row == 0, y_row(i), pltpu.roll(v, 1, 0))
        elif cy == -1:
            v = jnp.where(row == YS - 1, y_row(i), pltpu.roll(v, YS - 1, 0))
        if cz:
            v = pltpu.roll(v, cz % ZS, 1)
        reflected = mine[OPPOSITE[i]]
        wall = jnp.where(v > 0.0, reflected, 2.0 * WALL_DENSITY * WEIGHTS[i] - reflected)
        out.append(jnp.where(jnp.abs(v) < HALF_BIG, v, wall))
    return out


def fetch(hbm, vmem, sem):
    return [
        pltpu.make_async_copy(
            hbm.at[:, pl.ds(c * CHUNK, CHUNK)], vmem.at[:, pl.ds(1 + c * CHUNK, CHUNK)], sem.at[c]
        )
        for c in range(CHUNKS)
    ]


def place_x_halo(f, xlo, xhi):
    first = lax.axis_index("slab") == 0
    last = lax.axis_index("slab") == lax.axis_size("slab") - 1
    for k in range(5):
        f[X_UP[k], 0] = jnp.where(first, BIG, xlo[k])
        f[X_DOWN[k], XS + 1] = jnp.where(last, BIG, xhi[k])


def y_rows(ylo, yhi, x):
    first = lax.axis_index("blk") == 0
    last = lax.axis_index("blk") == lax.axis_size("blk") - 1

    def y_row(i):
        at = x + 1 - VELOCITIES[i][0]
        if i in Y_UP:
            return jnp.where(first, BIG, ylo[Y_UP.index(i), pl.ds(at, 1), :])
        return jnp.where(last, BIG, yhi[Y_DOWN.index(i), pl.ds(at, 1), :])

    return y_row


def prep_kernel(pops, solid, wetting, mark, xup, xdn, yup, ydn, x_planes, y_tiles, sem_x, sem_y):
    copies = []
    for k in range(5):
        copies.append(pltpu.make_async_copy(pops.at[X_UP[k], XS - 1], x_planes.at[k], sem_x.at[k]))
        copies.append(pltpu.make_async_copy(pops.at[X_DOWN[k], 0], x_planes.at[5 + k], sem_x.at[5 + k]))
        copies.append(pltpu.make_async_copy(pops.at[Y_UP[k], :, 8:16], y_tiles.at[k], sem_y.at[k]))
        copies.append(pltpu.make_async_copy(pops.at[Y_DOWN[k], :, 0:8], y_tiles.at[5 + k], sem_y.at[5 + k]))
    for copy in copies:
        copy.start()
    clear = jnp.zeros((YS, ZS), jnp.float32)
    mark[0] = clear
    mark[XS + 1] = clear
    for x in range(XS):
        mark[x + 1] = jnp.where(solid[x] == 1, jnp.where(wetting[x] == 1, -BIG, BIG), 0.0)
    for copy in copies:
        copy.wait()
    for k in range(5):
        for out, at, x in ((xup, k, XS), (xdn, 5 + k, 1)):
            m = mark[x]
            out[k] = jnp.where(m == 0.0, x_planes[at], m)
    for out, first, y in ((yup, 0, 7), (ydn, 5, 0)):
        m = mark[1 : XS + 1, y + (8 if first == 0 else 0), :]
        for k in range(5):
            out[k, 1 : XS + 1, :] = jnp.where(m == 0.0, y_tiles[first + k, :, y, :], m)


def step_one_kernel(pops, mark, xlo, xhi, ylo, yhi, out, xup, xdn, yup, ydn, f, res, sem_in, sem_out):
    copies = fetch(pops, f, sem_in)
    for copy in copies:
        copy.start()
    place_x_halo(f, xlo, xhi)
    def plane(x, carry):
        marked = {c: mark[x + 1 - c] for c in (-1, 0, 1)}

        def source(i):
            c = VELOCITIES[i][0]
            return jnp.where(marked[c] == 0.0, f[i, x + 1 - c], marked[c])

        pulled = pull(lambda i: f[i, x + 1], source, y_rows(ylo, yhi, x))
        new = collide(pulled)
        here = marked[0]
        for i in range(19):
            value = jnp.where(here == 0.0, new[i], here)
            res[i, x] = value
            if i in Y_UP:
                yup[Y_UP.index(i), pl.ds(x + 1, 1), :] = value[YS - 1 : YS]
            if i in Y_DOWN:
                ydn[Y_DOWN.index(i), pl.ds(x + 1, 1), :] = value[0:1]
        return carry

    outs = []
    copies[0].wait()
    for c in range(CHUNKS):
        if c + 1 < CHUNKS:
            copies[c + 1].wait()
        lax.fori_loop(c * CHUNK, (c + 1) * CHUNK, plane, 0)
        at = pl.ds(c * CHUNK, CHUNK)
        outs.append(pltpu.make_async_copy(res.at[:, at], out.at[:, at], sem_out.at[c]))
        outs[-1].start()
    for k in range(5):
        xup[k] = res[X_UP[k], XS - 1]
        xdn[k] = res[X_DOWN[k], 0]
    for copy in outs:
        copy.wait()


def step_two_kernel(owners, f1, xlo, xhi, ylo, yhi, outgoing, f, buf, absent, sem_in, sem_absent, sem_out):
    copies = fetch(f1, f, sem_in)
    for copy in copies:
        copy.start()
    absent[...] = jnp.full((8, ZS), -1.0, jnp.float32)
    label_rows = pl.ds(BLOCK_ROWS, 8)
    clears = [
        pltpu.make_async_copy(absent, outgoing.at[p, label_rows], sem_absent.at[p])
        for p in range(outgoing.shape[0])
    ]
    for clear in clears:
        clear.start()
    for k in range(BLOCKS):
        at = (k // 8 * 8 + 7 - k % 8) * SLOT_ROWS + BLOCK_ROWS
        buf[at : at + 8, :] = jnp.full((8, ZS), float(k), jnp.float32)
    place_x_halo(f, xlo, xhi)
    sub = lax.broadcasted_iota(jnp.int32, (8, ZS), 0)
    lane_block = lax.broadcasted_iota(jnp.int32, (8, ZS), 1) // 16
    pick = (lane_block + sub + 1) & 7

    def plane(x, carry):
        new = collide(
            pull(
                lambda i: f[i, x + 1],
                lambda i: f[i, x + 1 - VELOCITIES[i][0]],
                y_rows(ylo, yhi, x),
            )
        )
        fluid = jnp.abs(f[0, x + 1]) < HALF_BIG
        base = x // 16 * (8 * SLOT_ROWS) + x % 16 * 2
        for i in range(19):
            value = jnp.where(fluid, new[i], 0.0)
            for half in range(2):
                v = pltpu.roll(value[half * 8 : half * 8 + 8], 0, 1, stride=16, stride_axis=0)
                v = jnp.take_along_axis(v, pick, axis=0)
                v = pltpu.roll(v, 16, 1, stride=16, stride_axis=0)
                buf[pl.ds(base + i * 32 + half, 8, stride=SLOT_ROWS + 1), :] = v
        return carry

    outs = []
    copies[0].wait()
    for c in range(CHUNKS):
        if c + 1 < CHUNKS:
            copies[c + 1].wait()
        lax.fori_loop(c * CHUNK, (c + 1) * CHUNK, plane, 0)
        if c == 0:
            for clear in clears:
                clear.wait()
        if c % 4 == 3:
            for k in range(c // 4 * 8, c // 4 * 8 + 8):
                at = (k // 8 * 8 + 7 - k % 8) * SLOT_ROWS
                outs.append(
                    pltpu.make_async_copy(
                        buf.at[pl.ds(at, SLOT_ROWS)], outgoing.at[owners[k]], sem_out.at[k]
                    )
                )
                outs[-1].start()
    for copy in outs:
        copy.wait()


def place_kernel(incoming, out, labels, blocks, res, sem_label, sem_in, sem_out):
    peers = incoming.shape[0]
    copy = pltpu.make_async_copy(incoming.at[:, pl.ds(BLOCK_ROWS, 8)], labels, sem_label)
    copy.start()
    copy.wait()
    lane = lax.broadcasted_iota(jnp.int32, (1, ZS), 1)
    slot = lane.astype(jnp.float32)
    found = jnp.zeros((1, ZS), jnp.int32)
    for p in range(peers):
        found += jnp.where(labels[p, 7:8, :] == slot, p, 0)
    ins = []
    for k in range(BLOCKS):
        source = jnp.clip(jnp.sum(jnp.where(lane == k, found, 0)), 0, peers - 1)
        ins.append(
            pltpu.make_async_copy(
                incoming.at[source], blocks.at[pl.ds(k * SLOT_ROWS, SLOT_ROWS)], sem_in.at[k]
            )
        )
        ins[-1].start()
    outs = []
    for h in range(2):
        for k in range(8):
            ins[h * 8 + k].wait()

        def channel(i, carry):
            for j in range(32):
                at = h * 8 * SLOT_ROWS + 7 + i * 32 + j
                res[i, h * 8 : h * 8 + 8, j * 128 : (j + 1) * 128] = blocks[
                    pl.ds(at, 8, stride=SLOT_ROWS - 1), :
                ]
            return carry

        for part, (low, high) in enumerate(((0, 5), (5, 10), (10, 15), (15, 19))):
            lax.fori_loop(low, high, channel, 0)
            at = (pl.ds(low, high - low), pl.ds(h * 8, 8))
            outs.append(pltpu.make_async_copy(res.at[at], out.at[at], sem_out.at[h * 4 + part]))
            outs[-1].start()
    for copy in outs:
        copy.wait()


VMEM = pl.BlockSpec(memory_space=pltpu.VMEM)
ANY = pl.BlockSpec(memory_space=pl.ANY)
SMEM = pl.BlockSpec(memory_space=pltpu.SMEM)


def sds(*shape):
    return jax.ShapeDtypeStruct(shape, jnp.float32)


def params():
    return pltpu.CompilerParams(vmem_limit_bytes=48 * 1024 * 1024)


EDGES = (sds(5, YS, ZS), sds(5, YS, ZS), sds(5, HALO_ROWS, ZS), sds(5, HALO_ROWS, ZS))


def prep(pops, solid, wetting):
    return pl.pallas_call(
        prep_kernel,
        out_shape=(sds(XS + 2, YS, ZS), *EDGES),
        in_specs=[ANY, VMEM, VMEM],
        out_specs=(VMEM,) * 5,
        scratch_shapes=[
            pltpu.VMEM((10, YS, ZS), jnp.float32),
            pltpu.VMEM((10, XS, 8, ZS), jnp.float32),
            pltpu.SemaphoreType.DMA((10,)),
            pltpu.SemaphoreType.DMA((10,)),
        ],
        compiler_params=params(),
        name="prep",
    )(pops, solid, wetting)


def step_one(pops, mark, halo):
    return pl.pallas_call(
        step_one_kernel,
        out_shape=(sds(19, XS, YS, ZS), *EDGES),
        in_specs=[ANY] + [VMEM] * 5,
        out_specs=(ANY, VMEM, VMEM, VMEM, VMEM),
        scratch_shapes=[
            pltpu.VMEM((19, XS + 2, YS, ZS), jnp.float32),
            pltpu.VMEM((19, XS, YS, ZS), jnp.float32),
            pltpu.SemaphoreType.DMA((CHUNKS,)),
            pltpu.SemaphoreType.DMA((CHUNKS,)),
        ],
        compiler_params=params(),
        name="step_one",
    )(pops, mark, *halo)


def step_two(owners, f1, halo, peers):
    return pl.pallas_call(
        step_two_kernel,
        out_shape=sds(peers, SLOT_ROWS, ZS),
        in_specs=[SMEM, ANY] + [VMEM] * 4,
        out_specs=ANY,
        scratch_shapes=[
            pltpu.VMEM((19, XS + 2, YS, ZS), jnp.float32),
            pltpu.VMEM((BLOCKS * SLOT_ROWS, ZS), jnp.float32),
            pltpu.VMEM((8, ZS), jnp.float32),
            pltpu.SemaphoreType.DMA((CHUNKS,)),
            pltpu.SemaphoreType.DMA((peers,)),
            pltpu.SemaphoreType.DMA((BLOCKS,)),
        ],
        compiler_params=params(),
        name="step_two",
    )(owners, f1, *halo)


def place(incoming):
    peers = incoming.shape[0]
    return pl.pallas_call(
        place_kernel,
        out_shape=sds(19, BLOCKS, 4096),
        in_specs=[ANY],
        out_specs=ANY,
        scratch_shapes=[
            pltpu.VMEM((peers, 8, ZS), jnp.float32),
            pltpu.VMEM((BLOCKS * SLOT_ROWS, ZS), jnp.float32),
            pltpu.VMEM((19, BLOCKS, 4096), jnp.float32),
            pltpu.SemaphoreType.DMA,
            pltpu.SemaphoreType.DMA((BLOCKS,)),
            pltpu.SemaphoreType.DMA((8,)),
        ],
        compiler_params=params(),
        name="place",
    )(incoming)


def shift(value, axis, up):
    count = lax.axis_size(axis)
    steps = [(i, (i + 1) % count) if up else ((i + 1) % count, i) for i in range(count)]
    return lax.ppermute(value, axis, steps)


def exchange(xup, xdn, yup, ydn):
    xlo, xhi = shift(xup, "slab", True), shift(xdn, "slab", False)
    first = lax.axis_index("slab") == 0
    last = lax.axis_index("slab") == lax.axis_size("slab") - 1
    row = jnp.arange(HALO_ROWS)[:, None]

    def corners(rows, lo_channel, hi_channel, y, channels):
        parts = []
        for k, i in enumerate(channels):
            part = rows[k]
            if i == lo_channel:
                part = jnp.where(row == 0, jnp.where(first, BIG, xlo[X_UP.index(i), y]), part)
            if i == hi_channel:
                part = jnp.where(row == XS + 1, jnp.where(last, BIG, xhi[X_DOWN.index(i), y]), part)
            parts.append(part)
        return jnp.stack(parts)

    yup = corners(yup, 7, 10, YS - 1, Y_UP)
    ydn = corners(ydn, 9, 8, 0, Y_DOWN)
    return xlo, xhi, shift(yup, "blk", True), shift(ydn, "blk", False)


def per_device(populations, solid, wetting, dest):
    peers = lax.axis_size("blk")
    mark, *edges = prep(populations, solid, wetting)
    f1, *edges = step_one(populations, mark, exchange(*edges))
    outgoing = step_two(dest[0] // BLOCKS, f1, exchange(*edges), peers)
    incoming = lax.all_to_all(outgoing, "blk", split_axis=0, concat_axis=0, tiled=True)
    return place(incoming).transpose(1, 0, 2)


def solution(mesh):
    in_specs = (
        P(None, "slab", "blk", None),
        P("slab", "blk", None),
        P("slab", "blk", None),
        P("slab", "blk"),
    )
    out_specs = P(("slab", "blk"), None, None)
    return jax.shard_map(
        per_device, mesh=mesh, in_specs=in_specs, out_specs=out_specs, check_vma=False
    )
```

```python
import functools

import jax
import jax.numpy as jnp
import numpy as np
from jax import lax
from jax.experimental import pallas as pl
from jax.experimental.pallas import tpu as pltpu
from jax.sharding import PartitionSpec as P

VELOCITIES = [
    (0, 0, 0), (1, 0, 0), (-1, 0, 0), (0, 1, 0), (0, -1, 0), (0, 0, 1), (0, 0, -1),
    (1, 1, 0), (-1, -1, 0), (1, -1, 0), (-1, 1, 0), (1, 0, 1), (-1, 0, -1), (1, 0, -1),
    (-1, 0, 1), (0, 1, 1), (0, -1, -1), (0, 1, -1), (0, -1, 1),
]
OPPOSITE = [0, 2, 1, 4, 3, 6, 5, 8, 7, 10, 9, 12, 11, 14, 13, 16, 15, 18, 17]
WEIGHTS = [1.0 / 3.0] + [1.0 / 18.0] * 6 + [1.0 / 36.0] * 12
WALL_DENSITY = 1.2
BIG = 1e30
HALF_BIG = 1e29

X_UP = [i for i in range(19) if VELOCITIES[i][0] == 1]
X_DOWN = [i for i in range(19) if VELOCITIES[i][0] == -1]
Y_UP = [i for i in range(19) if VELOCITIES[i][1] == 1]
Y_DOWN = [i for i in range(19) if VELOCITIES[i][1] == -1]

XS, YS, ZS = 32, 16, 128
HALO_ROWS = 40
CHUNK = 4
CHUNKS = XS // CHUNK
BLOCKS = 16
BLOCK_ROWS = 19 * 32
SLOT_ROWS = BLOCK_ROWS + 8
PARTS = ((0, 10), (10, 19))


def collide(f):
    s, d = {}, {}
    for i in range(1, 19, 2):
        s[i] = f[i] + f[i + 1]
        d[i] = f[i] - f[i + 1]
    sxy, sxz, syz = s[7] + s[9], s[11] + s[13], s[15] + s[17]
    sx, sy, sz = s[1], s[3], s[5]
    rho = f[0] + (sx + sy) + (sz + sxy) + (sxz + syz)
    jx = d[1] + (d[7] + d[9]) + (d[11] + d[13])
    jy = d[3] + (d[7] - d[9]) + (d[15] + d[17])
    jz = d[5] + (d[11] - d[13]) + (d[15] - d[17])
    xx, yy, zz = jx * jx, jy * jy, jz * jz
    r = rho - 1.5 * (xx + yy + zz)
    tx, ty, tz = 2.0 * sx + 0.5 * xx, 2.0 * sy + 0.5 * yy, 2.0 * sz + 0.5 * zz
    base = 4.0 * f[0] - r
    qxy = (sxy - tx) + (base - ty + (xx + yy))
    qyz = (syz - ty) + (base - tz + (yy + zz))
    qxz = (sxz - tx) + (base - tz + (xx + zz))
    mean = (qxy + qyz + qxz) * (2.0 / 7.0)
    scale = 0.15 / 12.0
    a, b, c = (qxy - mean) * scale, (qyz - mean) * scale, (qxz - mean) * scale
    out = [None] * 19
    out[0] = -0.25 * f[0] + (1.25 / 3.0) * r - 4.0 * (a + b + c)
    axis_r = (1.25 / 18.0) * r
    plane_r = (1.25 / 36.0) * r

    def pair(i, along, square, even):
        w = WEIGHTS[i]
        e = even - 0.125 * s[i] + (1.25 * 4.5 * w) * square
        o = (1.6 * 3.0 * w) * along - 0.3 * d[i]
        out[i] = e + o
        out[i + 1] = e - o

    pair(1, jx, xx, axis_r + 2.0 * (a + c))
    pair(3, jy, yy, axis_r + 2.0 * (a + b))
    pair(5, jz, zz, axis_r + 2.0 * (b + c))
    for i, u, even in ((7, jx + jy, plane_r - a), (9, jx - jy, plane_r - a), (11, jx + jz, plane_r - c),
                       (13, jx - jz, plane_r - c), (15, jy + jz, plane_r - b), (17, jy - jz, plane_r - b)):
        pair(i, u, u * u, even)
    return out


def pull(own, source, y_row):
    row = lax.broadcasted_iota(jnp.int32, (YS, ZS), 0)
    mine = [own(i) for i in range(19)]
    out = [mine[0]]
    for i in range(1, 19):
        cx, cy, cz = VELOCITIES[i]
        v = source(i)
        if cy == 1:
            v = jnp.where(row == 0, y_row(i), pltpu.roll(v, 1, 0))
        elif cy == -1:
            v = jnp.where(row == YS - 1, y_row(i), pltpu.roll(v, YS - 1, 0))
        if cz:
            v = pltpu.roll(v, cz % ZS, 1)
        reflected = mine[OPPOSITE[i]]
        wall = jnp.where(v > 0.0, reflected, 2.0 * WALL_DENSITY * WEIGHTS[i] - reflected)
        out.append(jnp.where(jnp.abs(v) < HALF_BIG, v, wall))
    return out


def fetch(hbm, vmem, sem):
    return [
        pltpu.make_async_copy(
            hbm.at[:, pl.ds(c * CHUNK, CHUNK)], vmem.at[:, pl.ds(1 + c * CHUNK, CHUNK)], sem.at[c]
        )
        for c in range(CHUNKS)
    ]


def place_x_halo(f, xlo, xhi):
    first = lax.axis_index("slab") == 0
    last = lax.axis_index("slab") == lax.axis_size("slab") - 1
    for k in range(5):
        f[X_UP[k], 0] = jnp.where(first, BIG, xlo[k])
        f[X_DOWN[k], XS + 1] = jnp.where(last, BIG, xhi[k])


def y_rows(ylo, yhi, x):
    first = lax.axis_index("blk") == 0
    last = lax.axis_index("blk") == lax.axis_size("blk") - 1

    def y_row(i):
        at = x + 1 - VELOCITIES[i][0]
        if i in Y_UP:
            return jnp.where(first, BIG, ylo[Y_UP.index(i), pl.ds(at, 1), :])
        return jnp.where(last, BIG, yhi[Y_DOWN.index(i), pl.ds(at, 1), :])

    return y_row


def prep_kernel(pops, solid_in, wetting_in, mark, xup, xdn, yup, ydn, x_planes, y_tiles, solid, wetting, sem_x, sem_y, sem_k):
    kinds = [
        pltpu.make_async_copy(solid_in, solid, sem_k.at[0]),
        pltpu.make_async_copy(wetting_in, wetting, sem_k.at[1]),
    ]
    for copy in kinds:
        copy.start()
    copies = []
    for k in range(5):
        copies.append(pltpu.make_async_copy(pops.at[X_UP[k], XS - 1], x_planes.at[k], sem_x.at[k]))
        copies.append(pltpu.make_async_copy(pops.at[X_DOWN[k], 0], x_planes.at[5 + k], sem_x.at[5 + k]))
        copies.append(pltpu.make_async_copy(pops.at[Y_UP[k], :, 8:16], y_tiles.at[k], sem_y.at[k]))
        copies.append(pltpu.make_async_copy(pops.at[Y_DOWN[k], :, 0:8], y_tiles.at[5 + k], sem_y.at[5 + k]))
    for copy in copies:
        copy.start()
    clear = jnp.zeros((YS, ZS), jnp.float32)
    mark[0] = clear
    mark[XS + 1] = clear
    for copy in kinds:
        copy.wait()
    for x in range(XS):
        mark[x + 1] = jnp.where(solid[x] == 1, jnp.where(wetting[x] == 1, -BIG, BIG), 0.0)
    for copy in copies:
        copy.wait()
    for k in range(5):
        for out, at, x in ((xup, k, XS), (xdn, 5 + k, 1)):
            m = mark[x]
            out[k] = jnp.where(m == 0.0, x_planes[at], m)
    for out, first, y in ((yup, 0, 7), (ydn, 5, 0)):
        m = mark[1 : XS + 1, y + (8 if first == 0 else 0), :]
        for k in range(5):
            out[k, 1 : XS + 1, :] = jnp.where(m == 0.0, y_tiles[first + k, :, y, :], m)


def step_one_kernel(pops, mark_in, xlo, xhi, ylo, yhi, out, xup, xdn, yup, ydn, f, mark, res, sem_mark, sem_in, sem_out):
    mark_copy = pltpu.make_async_copy(mark_in, mark, sem_mark)
    mark_copy.start()
    copies = fetch(pops, f, sem_in)
    for copy in copies:
        copy.start()
    place_x_halo(f, xlo, xhi)
    def plane(x, carry):
        marked = {c: mark[x + 1 - c] for c in (-1, 0, 1)}

        def source(i):
            c = VELOCITIES[i][0]
            return jnp.where(marked[c] == 0.0, f[i, x + 1 - c], marked[c])

        pulled = pull(lambda i: f[i, x + 1], source, y_rows(ylo, yhi, x))
        new = collide(pulled)
        here = marked[0]
        for i in range(19):
            value = jnp.where(here == 0.0, new[i], here)
            res[i, x] = value
            if i in Y_UP:
                yup[Y_UP.index(i), pl.ds(x + 1, 1), :] = value[YS - 1 : YS]
            if i in Y_DOWN:
                ydn[Y_DOWN.index(i), pl.ds(x + 1, 1), :] = value[0:1]
        return carry

    outs = []
    mark_copy.wait()
    copies[0].wait()
    for c in range(CHUNKS):
        if c + 1 < CHUNKS:
            copies[c + 1].wait()
        lax.fori_loop(c * CHUNK, (c + 1) * CHUNK, plane, 0, unroll=2)
        at = pl.ds(c * CHUNK, CHUNK)
        outs.append(pltpu.make_async_copy(res.at[:, at], out.at[:, at], sem_out.at[c]))
        outs[-1].start()
    for k in range(5):
        xup[k] = res[X_UP[k], XS - 1]
        xdn[k] = res[X_DOWN[k], 0]
    for copy in outs:
        copy.wait()


def step_two_kernel(owners, f1, xlo, xhi, ylo, yhi, outgoing, f, buf, absent, sem_in, sem_absent, sem_out):
    copies = fetch(f1, f, sem_in)
    for copy in copies:
        copy.start()
    absent[...] = jnp.full((8, ZS), -1.0, jnp.float32)
    label_rows = pl.ds(BLOCK_ROWS, 8)
    clears = [
        pltpu.make_async_copy(absent, outgoing.at[p, label_rows], sem_absent.at[p])
        for p in range(outgoing.shape[0])
    ]
    for clear in clears:
        clear.start()
    for k in range(BLOCKS):
        at = (k // 8 * 8 + 7 - k % 8) * SLOT_ROWS + BLOCK_ROWS
        buf[at : at + 8, :] = jnp.full((8, ZS), float(k), jnp.float32)
    place_x_halo(f, xlo, xhi)
    sub = lax.broadcasted_iota(jnp.int32, (8, ZS), 0)
    lane_block = lax.broadcasted_iota(jnp.int32, (8, ZS), 1) // 16
    pick = (lane_block + sub + 1) & 7

    def plane(x, carry):
        new = collide(
            pull(
                lambda i: f[i, x + 1],
                lambda i: f[i, x + 1 - VELOCITIES[i][0]],
                y_rows(ylo, yhi, x),
            )
        )
        fluid = jnp.abs(f[0, x + 1]) < HALF_BIG
        base = x // 16 * (8 * SLOT_ROWS) + x % 16 * 2
        tiles = []
        for i in range(19):
            value = jnp.where(fluid, new[i], 0.0)
            tiles += [(i * 32 + half, value[half * 8 : half * 8 + 8]) for half in range(2)]
        tiles = [(at, pltpu.roll(v, 0, 1, stride=16, stride_axis=0)) for at, v in tiles]
        tiles = [(at, jnp.take_along_axis(v, pick, axis=0)) for at, v in tiles]
        tiles = [(at, pltpu.roll(v, 16, 1, stride=16, stride_axis=0)) for at, v in tiles]
        for at, v in tiles:
            buf[pl.ds(base + at, 8, stride=SLOT_ROWS), :] = v
        return carry

    outs = []
    copies[0].wait()
    for c in range(CHUNKS):
        if c + 1 < CHUNKS:
            copies[c + 1].wait()
        lax.fori_loop(c * CHUNK, (c + 1) * CHUNK, plane, 0, unroll=2)
        if c == 0:
            for clear in clears:
                clear.wait()
        if c % 4 == 3:
            for k in range(c // 4 * 8, c // 4 * 8 + 8):
                at = (k // 8 * 8 + 7 - k % 8) * SLOT_ROWS
                outs.append(
                    pltpu.make_async_copy(
                        buf.at[pl.ds(at, SLOT_ROWS)], outgoing.at[owners[k]], sem_out.at[k]
                    )
                )
                outs[-1].start()
    for copy in outs:
        copy.wait()


def place_kernel(incoming, out, labels, blocks, res, sem_label, sem_in, sem_out):
    peers = incoming.shape[0]
    copy = pltpu.make_async_copy(incoming.at[:, pl.ds(BLOCK_ROWS, 8)], labels, sem_label)
    copy.start()
    copy.wait()
    lane = lax.broadcasted_iota(jnp.int32, (1, ZS), 1)
    slot = lane.astype(jnp.float32)
    found = jnp.zeros((1, ZS), jnp.int32)
    for p in range(peers):
        found += jnp.where(labels[p, 7:8, :] == slot, p, 0)
    found = jnp.clip(found, 0, peers - 1)
    sources = [found[0, k] for k in range(BLOCKS)]
    ins = []
    for part, (low, high) in enumerate(PARTS):
        for k in range(BLOCKS):
            rows = (high - low) * 32
            ins.append(
                pltpu.make_async_copy(
                    incoming.at[sources[k], pl.ds(low * 32, rows)],
                    blocks.at[pl.ds(k * SLOT_ROWS + low * 32, rows)],
                    sem_in.at[part * BLOCKS + k],
                )
            )
            ins[-1].start()
    outs = []

    def channel(i, carry):
        for h in range(2):
            for j in range(32):
                at = h * 8 * SLOT_ROWS + i * 32 + j
                res[i, h * 8 : h * 8 + 8, j * 128 : (j + 1) * 128] = blocks[
                    pl.ds(at, 8, stride=SLOT_ROWS), :
                ]
        return carry

    for part, (low, high) in enumerate(PARTS):
        for k in range(BLOCKS):
            ins[part * BLOCKS + k].wait()
        lax.fori_loop(low, high, channel, 0)
        at = pl.ds(low, high - low)
        outs.append(pltpu.make_async_copy(res.at[at], out.at[at], sem_out.at[part]))
        outs[-1].start()
    for copy in outs:
        copy.wait()


VMEM = pl.BlockSpec(memory_space=pltpu.VMEM)
ANY = pl.BlockSpec(memory_space=pl.ANY)
SMEM = pl.BlockSpec(memory_space=pltpu.SMEM)


def sds(*shape):
    return jax.ShapeDtypeStruct(shape, jnp.float32)


def params(mib=48):
    return pltpu.CompilerParams(vmem_limit_bytes=mib * 1024 * 1024)


EDGES = (sds(5, YS, ZS), sds(5, YS, ZS), sds(5, HALO_ROWS, ZS), sds(5, HALO_ROWS, ZS))


def prep(pops, solid, wetting):
    return pl.pallas_call(
        prep_kernel,
        out_shape=(sds(XS + 2, YS, ZS), *EDGES),
        in_specs=[ANY, ANY, ANY],
        out_specs=(VMEM,) * 5,
        scratch_shapes=[
            pltpu.VMEM((10, YS, ZS), jnp.float32),
            pltpu.VMEM((10, XS, 8, ZS), jnp.float32),
            pltpu.VMEM((XS, YS, ZS), jnp.int32),
            pltpu.VMEM((XS, YS, ZS), jnp.int32),
            pltpu.SemaphoreType.DMA((10,)),
            pltpu.SemaphoreType.DMA((10,)),
            pltpu.SemaphoreType.DMA((2,)),
        ],
        compiler_params=params(60),
        name="prep",
    )(pops, solid, wetting)


def step_one(pops, mark, halo):
    return pl.pallas_call(
        step_one_kernel,
        out_shape=(sds(19, XS, YS, ZS), *EDGES),
        in_specs=[ANY, ANY] + [VMEM] * 4,
        out_specs=(ANY, VMEM, VMEM, VMEM, VMEM),
        scratch_shapes=[
            pltpu.VMEM((19, XS + 2, YS, ZS), jnp.float32),
            pltpu.VMEM((XS + 2, YS, ZS), jnp.float32),
            pltpu.VMEM((19, XS, YS, ZS), jnp.float32),
            pltpu.SemaphoreType.DMA,
            pltpu.SemaphoreType.DMA((CHUNKS,)),
            pltpu.SemaphoreType.DMA((CHUNKS,)),
        ],
        compiler_params=params(),
        name="step_one",
    )(pops, mark, *halo)


def step_two(owners, f1, halo, peers):
    return pl.pallas_call(
        step_two_kernel,
        out_shape=sds(peers, SLOT_ROWS, ZS),
        in_specs=[SMEM, ANY] + [VMEM] * 4,
        out_specs=ANY,
        scratch_shapes=[
            pltpu.VMEM((19, XS + 2, YS, ZS), jnp.float32),
            pltpu.VMEM((BLOCKS * SLOT_ROWS, ZS), jnp.float32),
            pltpu.VMEM((8, ZS), jnp.float32),
            pltpu.SemaphoreType.DMA((CHUNKS,)),
            pltpu.SemaphoreType.DMA((peers,)),
            pltpu.SemaphoreType.DMA((BLOCKS,)),
        ],
        compiler_params=params(),
        name="step_two",
    )(owners, f1, *halo)


def place(incoming):
    peers = incoming.shape[0]
    return pl.pallas_call(
        place_kernel,
        out_shape=sds(19, BLOCKS, 4096),
        in_specs=[ANY],
        out_specs=ANY,
        scratch_shapes=[
            pltpu.VMEM((peers, 8, ZS), jnp.float32),
            pltpu.VMEM((BLOCKS * SLOT_ROWS, ZS), jnp.float32),
            pltpu.VMEM((19, BLOCKS, 4096), jnp.float32),
            pltpu.SemaphoreType.DMA,
            pltpu.SemaphoreType.DMA((len(PARTS) * BLOCKS,)),
            pltpu.SemaphoreType.DMA((len(PARTS),)),
        ],
        compiler_params=params(),
        name="place",
    )(incoming)


def shift(value, axis, up):
    count = lax.axis_size(axis)
    steps = [(i, (i + 1) % count) if up else ((i + 1) % count, i) for i in range(count)]
    return lax.ppermute(value, axis, steps)


def exchange(xup, xdn, yup, ydn):
    xlo, xhi = shift(xup, "slab", True), shift(xdn, "slab", False)
    first = lax.axis_index("slab") == 0
    last = lax.axis_index("slab") == lax.axis_size("slab") - 1
    row = jnp.arange(HALO_ROWS)[:, None]

    def corners(rows, lo_channel, hi_channel, y, channels):
        parts = []
        for k, i in enumerate(channels):
            part = rows[k]
            if i == lo_channel:
                part = jnp.where(row == 0, jnp.where(first, BIG, xlo[X_UP.index(i), y]), part)
            if i == hi_channel:
                part = jnp.where(row == XS + 1, jnp.where(last, BIG, xhi[X_DOWN.index(i), y]), part)
            parts.append(part)
        return jnp.stack(parts)

    yup = corners(yup, 7, 10, YS - 1, Y_UP)
    ydn = corners(ydn, 9, 8, 0, Y_DOWN)
    return xlo, xhi, shift(yup, "blk", True), shift(ydn, "blk", False)


def per_device(populations, solid, wetting, dest):
    peers = lax.axis_size("blk")
    mark, *edges = prep(populations, solid, wetting)
    f1, *edges = step_one(populations, mark, exchange(*edges))
    outgoing = step_two(dest[0] // BLOCKS, f1, exchange(*edges), peers)
    incoming = lax.all_to_all(outgoing, "blk", split_axis=0, concat_axis=0, tiled=True)
    return place(incoming).transpose(1, 0, 2)


def solution(mesh):
    in_specs = (
        P(None, "slab", "blk", None),
        P("slab", "blk", None),
        P("slab", "blk", None),
        P("slab", "blk"),
    )
    out_specs = P(("slab", "blk"), None, None)
    return jax.shard_map(
        per_device, mesh=mesh, in_specs=in_specs, out_specs=out_specs, check_vma=False
    )
```

```python
import functools

import jax
import jax.numpy as jnp
import numpy as np
from jax import lax
from jax.experimental import pallas as pl
from jax.experimental.pallas import tpu as pltpu
from jax.sharding import PartitionSpec as P

VELOCITIES = [
    (0, 0, 0), (1, 0, 0), (-1, 0, 0), (0, 1, 0), (0, -1, 0), (0, 0, 1), (0, 0, -1),
    (1, 1, 0), (-1, -1, 0), (1, -1, 0), (-1, 1, 0), (1, 0, 1), (-1, 0, -1), (1, 0, -1),
    (-1, 0, 1), (0, 1, 1), (0, -1, -1), (0, 1, -1), (0, -1, 1),
]
OPPOSITE = [0, 2, 1, 4, 3, 6, 5, 8, 7, 10, 9, 12, 11, 14, 13, 16, 15, 18, 17]
WEIGHTS = [1.0 / 3.0] + [1.0 / 18.0] * 6 + [1.0 / 36.0] * 12
WALL_DENSITY = 1.2
BIG = 1e30
HALF_BIG = 1e29

X_UP = [i for i in range(19) if VELOCITIES[i][0] == 1]
X_DOWN = [i for i in range(19) if VELOCITIES[i][0] == -1]
Y_UP = [i for i in range(19) if VELOCITIES[i][1] == 1]
Y_DOWN = [i for i in range(19) if VELOCITIES[i][1] == -1]

XS, YS, ZS = 32, 16, 128
HALO_ROWS = 40
CHUNK = 4
CHUNKS = XS // CHUNK
BLOCKS = 16
BLOCK_ROWS = 19 * 32
SLOT_ROWS = BLOCK_ROWS + 8


def collide(f):
    s, d = {}, {}
    for i in range(1, 19, 2):
        s[i] = f[i] + f[i + 1]
        d[i] = f[i] - f[i + 1]
    sxy, sxz, syz = s[7] + s[9], s[11] + s[13], s[15] + s[17]
    sx, sy, sz = s[1], s[3], s[5]
    rho = f[0] + (sx + sy) + (sz + sxy) + (sxz + syz)
    jx = d[1] + (d[7] + d[9]) + (d[11] + d[13])
    jy = d[3] + (d[7] - d[9]) + (d[15] + d[17])
    jz = d[5] + (d[11] - d[13]) + (d[15] - d[17])
    xx, yy, zz = jx * jx, jy * jy, jz * jz
    r = rho - 1.5 * (xx + yy + zz)
    tx, ty, tz = 2.0 * sx + 0.5 * xx, 2.0 * sy + 0.5 * yy, 2.0 * sz + 0.5 * zz
    base = 4.0 * f[0] - r
    qxy = (sxy - tx) + (base - ty + (xx + yy))
    qyz = (syz - ty) + (base - tz + (yy + zz))
    qxz = (sxz - tx) + (base - tz + (xx + zz))
    mean = (qxy + qyz + qxz) * (2.0 / 7.0)
    scale = 0.15 / 12.0
    a, b, c = (qxy - mean) * scale, (qyz - mean) * scale, (qxz - mean) * scale
    out = [None] * 19
    out[0] = -0.25 * f[0] + (1.25 / 3.0) * r - 4.0 * (a + b + c)
    axis_r = (1.25 / 18.0) * r
    plane_r = (1.25 / 36.0) * r

    def pair(i, along, square, even):
        w = WEIGHTS[i]
        e = even - 0.125 * s[i] + (1.25 * 4.5 * w) * square
        o = (1.6 * 3.0 * w) * along - 0.3 * d[i]
        out[i] = e + o
        out[i + 1] = e - o

    pair(1, jx, xx, axis_r + 2.0 * (a + c))
    pair(3, jy, yy, axis_r + 2.0 * (a + b))
    pair(5, jz, zz, axis_r + 2.0 * (b + c))
    for i, u, even in ((7, jx + jy, plane_r - a), (9, jx - jy, plane_r - a), (11, jx + jz, plane_r - c),
                       (13, jx - jz, plane_r - c), (15, jy + jz, plane_r - b), (17, jy - jz, plane_r - b)):
        pair(i, u, u * u, even)
    return out


def pull(own, source, y_row):
    row = lax.broadcasted_iota(jnp.int32, (YS, ZS), 0)
    mine = [own(i) for i in range(19)]
    out = [mine[0]]
    for i in range(1, 19):
        cx, cy, cz = VELOCITIES[i]
        v = source(i)
        if cy == 1:
            v = jnp.where(row == 0, y_row(i), pltpu.roll(v, 1, 0))
        elif cy == -1:
            v = jnp.where(row == YS - 1, y_row(i), pltpu.roll(v, YS - 1, 0))
        if cz:
            v = pltpu.roll(v, cz % ZS, 1)
        reflected = mine[OPPOSITE[i]]
        wall = jnp.where(v > 0.0, reflected, 2.0 * WALL_DENSITY * WEIGHTS[i] - reflected)
        out.append(jnp.where(jnp.abs(v) < HALF_BIG, v, wall))
    return out


def fetch(hbm, vmem, sem):
    return [
        pltpu.make_async_copy(
            hbm.at[:, pl.ds(c * CHUNK, CHUNK)], vmem.at[:, pl.ds(1 + c * CHUNK, CHUNK)], sem.at[c]
        )
        for c in range(CHUNKS)
    ]


def place_x_halo(f, xlo, xhi):
    first = lax.axis_index("slab") == 0
    last = lax.axis_index("slab") == lax.axis_size("slab") - 1
    for k in range(5):
        f[X_UP[k], 0] = jnp.where(first, BIG, xlo[k])
        f[X_DOWN[k], XS + 1] = jnp.where(last, BIG, xhi[k])


def y_rows(ylo, yhi, x):
    first = lax.axis_index("blk") == 0
    last = lax.axis_index("blk") == lax.axis_size("blk") - 1

    def y_row(i):
        at = x + 1 - VELOCITIES[i][0]
        if i in Y_UP:
            return jnp.where(first, BIG, ylo[Y_UP.index(i), pl.ds(at, 1), :])
        return jnp.where(last, BIG, yhi[Y_DOWN.index(i), pl.ds(at, 1), :])

    return y_row


def prep_kernel(pops, mark, xup, xdn, yup, ydn, x_planes, y_tiles, sem_x, sem_y):
    copies = []
    for k in range(5):
        copies.append(pltpu.make_async_copy(pops.at[X_UP[k], XS - 1], x_planes.at[k], sem_x.at[k]))
        copies.append(pltpu.make_async_copy(pops.at[X_DOWN[k], 0], x_planes.at[5 + k], sem_x.at[5 + k]))
        copies.append(pltpu.make_async_copy(pops.at[Y_UP[k], :, 8:16], y_tiles.at[k], sem_y.at[k]))
        copies.append(pltpu.make_async_copy(pops.at[Y_DOWN[k], :, 0:8], y_tiles.at[5 + k], sem_y.at[5 + k]))
    for copy in copies:
        copy.start()
    for copy in copies:
        copy.wait()
    for k in range(5):
        for out, at, x in ((xup, k, XS - 1), (xdn, 5 + k, 0)):
            m = mark[x]
            out[k] = jnp.where(m == 0.0, x_planes[at], m)
    for out, first, y in ((yup, 0, 7), (ydn, 5, 0)):
        m = mark[:, y + (8 if first == 0 else 0), :]
        for k in range(5):
            out[k, 1 : XS + 1, :] = jnp.where(m == 0.0, y_tiles[first + k, :, y, :], m)


def step_one_kernel(pops, mark, xlo, xhi, ylo, yhi, out, xup, xdn, yup, ydn, f, res, sem_in, sem_out):
    copies = fetch(pops, f, sem_in)
    for copy in copies:
        copy.start()
    place_x_halo(f, xlo, xhi)
    def plane(x, carry):
        marked = {
            0: mark[x],
            1: jnp.where(x == 0, 0.0, mark[jnp.maximum(x - 1, 0)]),
            -1: jnp.where(x == XS - 1, 0.0, mark[jnp.minimum(x + 1, XS - 1)]),
        }

        def source(i):
            c = VELOCITIES[i][0]
            return jnp.where(marked[c] == 0.0, f[i, x + 1 - c], marked[c])

        pulled = pull(lambda i: f[i, x + 1], source, y_rows(ylo, yhi, x))
        new = collide(pulled)
        here = marked[0]
        for i in range(19):
            value = jnp.where(here == 0.0, new[i], here)
            res[i, x] = value
            if i in Y_UP:
                yup[Y_UP.index(i), pl.ds(x + 1, 1), :] = value[YS - 1 : YS]
            if i in Y_DOWN:
                ydn[Y_DOWN.index(i), pl.ds(x + 1, 1), :] = value[0:1]
        return carry

    outs = []
    copies[0].wait()
    for c in range(CHUNKS):
        if c + 1 < CHUNKS:
            copies[c + 1].wait()
        lax.fori_loop(c * CHUNK, (c + 1) * CHUNK, plane, 0, unroll=2)
        at = pl.ds(c * CHUNK, CHUNK)
        outs.append(pltpu.make_async_copy(res.at[:, at], out.at[:, at], sem_out.at[c]))
        outs[-1].start()
    for k in range(5):
        xup[k] = res[X_UP[k], XS - 1]
        xdn[k] = res[X_DOWN[k], 0]
    for copy in outs:
        copy.wait()


def step_two_kernel(owners, f1, xlo, xhi, ylo, yhi, outgoing, f, buf, absent, sem_in, sem_absent, sem_out):
    copies = fetch(f1, f, sem_in)
    for copy in copies:
        copy.start()
    absent[...] = jnp.full((8, ZS), -1.0, jnp.float32)
    label_rows = pl.ds(BLOCK_ROWS, 8)
    clears = [
        pltpu.make_async_copy(absent, outgoing.at[p, label_rows], sem_absent.at[p])
        for p in range(outgoing.shape[0])
    ]
    for clear in clears:
        clear.start()
    for k in range(BLOCKS):
        at = (k // 8 * 8 + 7 - k % 8) * SLOT_ROWS + BLOCK_ROWS
        buf[at : at + 8, :] = jnp.full((8, ZS), float(k), jnp.float32)
    place_x_halo(f, xlo, xhi)
    sub = lax.broadcasted_iota(jnp.int32, (8, ZS), 0)
    lane_block = lax.broadcasted_iota(jnp.int32, (8, ZS), 1) // 16
    pick = (lane_block + sub + 1) & 7

    def plane(x, carry):
        new = collide(
            pull(
                lambda i: f[i, x + 1],
                lambda i: f[i, x + 1 - VELOCITIES[i][0]],
                y_rows(ylo, yhi, x),
            )
        )
        fluid = jnp.abs(f[0, x + 1]) < HALF_BIG
        base = x // 16 * (8 * SLOT_ROWS) + x % 16 * 2
        tiles = []
        for i in range(19):
            value = jnp.where(fluid, new[i], 0.0)
            tiles += [(i * 32 + half, value[half * 8 : half * 8 + 8]) for half in range(2)]
        tiles = [(at, pltpu.roll(v, 0, 1, stride=16, stride_axis=0)) for at, v in tiles]
        tiles = [(at, jnp.take_along_axis(v, pick, axis=0)) for at, v in tiles]
        tiles = [(at, pltpu.roll(v, 16, 1, stride=16, stride_axis=0)) for at, v in tiles]
        for at, v in tiles:
            buf[pl.ds(base + at, 8, stride=SLOT_ROWS), :] = v
        return carry

    outs = []
    copies[0].wait()
    for c in range(CHUNKS):
        if c + 1 < CHUNKS:
            copies[c + 1].wait()
        lax.fori_loop(c * CHUNK, (c + 1) * CHUNK, plane, 0, unroll=2)
        if c == 0:
            for clear in clears:
                clear.wait()
        if c % 4 == 3:
            for k in range(c // 4 * 8, c // 4 * 8 + 8):
                at = (k // 8 * 8 + 7 - k % 8) * SLOT_ROWS
                outs.append(
                    pltpu.make_async_copy(
                        buf.at[pl.ds(at, SLOT_ROWS)], outgoing.at[owners[k]], sem_out.at[k]
                    )
                )
                outs[-1].start()
    for copy in outs:
        copy.wait()


def place_kernel(incoming, out, labels, blocks, res, sem_label, sem_in, sem_out):
    peers = incoming.shape[0]
    copy = pltpu.make_async_copy(incoming.at[:, pl.ds(BLOCK_ROWS, 8)], labels, sem_label)
    copy.start()
    copy.wait()
    lane = lax.broadcasted_iota(jnp.int32, (1, ZS), 1)
    slot = lane.astype(jnp.float32)
    found = jnp.zeros((1, ZS), jnp.int32)
    for p in range(peers):
        found += jnp.where(labels[p, 7:8, :] == slot, p, 0)
    ins = []
    for k in range(BLOCKS):
        source = jnp.clip(jnp.sum(jnp.where(lane == k, found, 0)), 0, peers - 1)
        ins.append(
            pltpu.make_async_copy(
                incoming.at[source], blocks.at[pl.ds(k * SLOT_ROWS, SLOT_ROWS)], sem_in.at[k]
            )
        )
        ins[-1].start()
    outs = []
    for h in range(2):
        for k in range(8):
            ins[h * 8 + k].wait()

        def channel(i, carry):
            for j in range(32):
                at = h * 8 * SLOT_ROWS + i * 32 + j
                res[i, h * 8 : h * 8 + 8, j * 128 : (j + 1) * 128] = blocks[
                    pl.ds(at, 8, stride=SLOT_ROWS), :
                ]
            return carry

        for part, (low, high) in enumerate(((0, 5), (5, 10), (10, 15), (15, 19))):
            lax.fori_loop(low, high, channel, 0)
            at = (pl.ds(low, high - low), pl.ds(h * 8, 8))
            outs.append(pltpu.make_async_copy(res.at[at], out.at[at], sem_out.at[h * 4 + part]))
            outs[-1].start()
    for copy in outs:
        copy.wait()


VMEM = pl.BlockSpec(memory_space=pltpu.VMEM)
ANY = pl.BlockSpec(memory_space=pl.ANY)
SMEM = pl.BlockSpec(memory_space=pltpu.SMEM)


def sds(*shape):
    return jax.ShapeDtypeStruct(shape, jnp.float32)


def params(mib=48):
    return pltpu.CompilerParams(vmem_limit_bytes=mib * 1024 * 1024)


EDGES = (sds(5, YS, ZS), sds(5, YS, ZS), sds(5, HALO_ROWS, ZS), sds(5, HALO_ROWS, ZS))


def prep(pops, mark):
    return pl.pallas_call(
        prep_kernel,
        out_shape=EDGES,
        in_specs=[ANY, VMEM],
        out_specs=(VMEM,) * 4,
        scratch_shapes=[
            pltpu.VMEM((10, YS, ZS), jnp.float32),
            pltpu.VMEM((10, XS, 8, ZS), jnp.float32),
            pltpu.SemaphoreType.DMA((10,)),
            pltpu.SemaphoreType.DMA((10,)),
        ],
        compiler_params=params(50),
        name="prep",
    )(pops, mark)


def step_one(pops, mark, halo):
    return pl.pallas_call(
        step_one_kernel,
        out_shape=(sds(19, XS, YS, ZS), *EDGES),
        in_specs=[ANY] + [VMEM] * 5,
        out_specs=(ANY, VMEM, VMEM, VMEM, VMEM),
        scratch_shapes=[
            pltpu.VMEM((19, XS + 2, YS, ZS), jnp.float32),
            pltpu.VMEM((19, XS, YS, ZS), jnp.float32),
            pltpu.SemaphoreType.DMA((CHUNKS,)),
            pltpu.SemaphoreType.DMA((CHUNKS,)),
        ],
        compiler_params=params(),
        name="step_one",
    )(pops, mark, *halo)


def step_two(owners, f1, halo, peers):
    return pl.pallas_call(
        step_two_kernel,
        out_shape=sds(peers, SLOT_ROWS, ZS),
        in_specs=[SMEM, ANY] + [VMEM] * 4,
        out_specs=ANY,
        scratch_shapes=[
            pltpu.VMEM((19, XS + 2, YS, ZS), jnp.float32),
            pltpu.VMEM((BLOCKS * SLOT_ROWS, ZS), jnp.float32),
            pltpu.VMEM((8, ZS), jnp.float32),
            pltpu.SemaphoreType.DMA((CHUNKS,)),
            pltpu.SemaphoreType.DMA((peers,)),
            pltpu.SemaphoreType.DMA((BLOCKS,)),
        ],
        compiler_params=params(),
        name="step_two",
    )(owners, f1, *halo)


def place(incoming):
    peers = incoming.shape[0]
    return pl.pallas_call(
        place_kernel,
        out_shape=sds(19, BLOCKS, 4096),
        in_specs=[ANY],
        out_specs=ANY,
        scratch_shapes=[
            pltpu.VMEM((peers, 8, ZS), jnp.float32),
            pltpu.VMEM((BLOCKS * SLOT_ROWS, ZS), jnp.float32),
            pltpu.VMEM((19, BLOCKS, 4096), jnp.float32),
            pltpu.SemaphoreType.DMA,
            pltpu.SemaphoreType.DMA((BLOCKS,)),
            pltpu.SemaphoreType.DMA((8,)),
        ],
        compiler_params=params(),
        name="place",
    )(incoming)


def shift(value, axis, up):
    count = lax.axis_size(axis)
    steps = [(i, (i + 1) % count) if up else ((i + 1) % count, i) for i in range(count)]
    return lax.ppermute(value, axis, steps)


def exchange(xup, xdn, yup, ydn):
    xlo, xhi = shift(xup, "slab", True), shift(xdn, "slab", False)
    first = lax.axis_index("slab") == 0
    last = lax.axis_index("slab") == lax.axis_size("slab") - 1
    row = jnp.arange(HALO_ROWS)[:, None]

    def corners(rows, lo_channel, hi_channel, y, channels):
        parts = []
        for k, i in enumerate(channels):
            part = rows[k]
            if i == lo_channel:
                part = jnp.where(row == 0, jnp.where(first, BIG, xlo[X_UP.index(i), y]), part)
            if i == hi_channel:
                part = jnp.where(row == XS + 1, jnp.where(last, BIG, xhi[X_DOWN.index(i), y]), part)
            parts.append(part)
        return jnp.stack(parts)

    yup = corners(yup, 7, 10, YS - 1, Y_UP)
    ydn = corners(ydn, 9, 8, 0, Y_DOWN)
    return xlo, xhi, shift(yup, "blk", True), shift(ydn, "blk", False)


def per_device(populations, solid, wetting, dest):
    peers = lax.axis_size("blk")
    mark = jnp.where(solid == 1, jnp.where(wetting == 1, -BIG, BIG), 0.0)
    edges = prep(populations, mark)
    f1, *edges = step_one(populations, mark, exchange(*edges))
    outgoing = step_two(dest[0] // BLOCKS, f1, exchange(*edges), peers)
    incoming = lax.all_to_all(outgoing, "blk", split_axis=0, concat_axis=0, tiled=True)
    return place(incoming).transpose(1, 0, 2)


def solution(mesh):
    in_specs = (
        P(None, "slab", "blk", None),
        P("slab", "blk", None),
        P("slab", "blk", None),
        P("slab", "blk"),
    )
    out_specs = P(("slab", "blk"), None, None)
    return jax.shard_map(
        per_device, mesh=mesh, in_specs=in_specs, out_specs=out_specs, check_vma=False
    )
```

```python
import functools

import jax
import jax.numpy as jnp
import numpy as np
from jax import lax
from jax.experimental import pallas as pl
from jax.experimental.pallas import tpu as pltpu
from jax.sharding import PartitionSpec as P

VELOCITIES = [
    (0, 0, 0), (1, 0, 0), (-1, 0, 0), (0, 1, 0), (0, -1, 0), (0, 0, 1), (0, 0, -1),
    (1, 1, 0), (-1, -1, 0), (1, -1, 0), (-1, 1, 0), (1, 0, 1), (-1, 0, -1), (1, 0, -1),
    (-1, 0, 1), (0, 1, 1), (0, -1, -1), (0, 1, -1), (0, -1, 1),
]
OPPOSITE = [0, 2, 1, 4, 3, 6, 5, 8, 7, 10, 9, 12, 11, 14, 13, 16, 15, 18, 17]
WEIGHTS = [1.0 / 3.0] + [1.0 / 18.0] * 6 + [1.0 / 36.0] * 12
WALL_DENSITY = 1.2
BIG = 1e30
HALF_BIG = 1e29

X_UP = [i for i in range(19) if VELOCITIES[i][0] == 1]
X_DOWN = [i for i in range(19) if VELOCITIES[i][0] == -1]
Y_UP = [i for i in range(19) if VELOCITIES[i][1] == 1]
Y_DOWN = [i for i in range(19) if VELOCITIES[i][1] == -1]

XS, YS, ZS = 32, 16, 128
HALO_ROWS = 40
CHUNK = 4
CHUNKS = XS // CHUNK
BLOCKS = 16
BLOCK_ROWS = 19 * 32
SLOT_ROWS = BLOCK_ROWS + 8
CHUNK_ROWS = 19 * 2 * CHUNK


def collide(f):
    s, d = {}, {}
    for i in range(1, 19, 2):
        s[i] = f[i] + f[i + 1]
        d[i] = f[i] - f[i + 1]
    sxy, sxz, syz = s[7] + s[9], s[11] + s[13], s[15] + s[17]
    sx, sy, sz = s[1], s[3], s[5]
    rho = f[0] + (sx + sy) + (sz + sxy) + (sxz + syz)
    jx = d[1] + (d[7] + d[9]) + (d[11] + d[13])
    jy = d[3] + (d[7] - d[9]) + (d[15] + d[17])
    jz = d[5] + (d[11] - d[13]) + (d[15] - d[17])
    xx, yy, zz = jx * jx, jy * jy, jz * jz
    r = rho - 1.5 * (xx + yy + zz)
    tx, ty, tz = 2.0 * sx + 0.5 * xx, 2.0 * sy + 0.5 * yy, 2.0 * sz + 0.5 * zz
    base = 4.0 * f[0] - r
    qxy = (sxy - tx) + (base - ty + (xx + yy))
    qyz = (syz - ty) + (base - tz + (yy + zz))
    qxz = (sxz - tx) + (base - tz + (xx + zz))
    mean = (qxy + qyz + qxz) * (2.0 / 7.0)
    scale = 0.15 / 12.0
    a, b, c = (qxy - mean) * scale, (qyz - mean) * scale, (qxz - mean) * scale
    out = [None] * 19
    out[0] = -0.25 * f[0] + (1.25 / 3.0) * r - 4.0 * (a + b + c)
    axis_r = (1.25 / 18.0) * r
    plane_r = (1.25 / 36.0) * r

    def pair(i, along, square, even):
        w = WEIGHTS[i]
        e = even - 0.125 * s[i] + (1.25 * 4.5 * w) * square
        o = (1.6 * 3.0 * w) * along - 0.3 * d[i]
        out[i] = e + o
        out[i + 1] = e - o

    pair(1, jx, xx, axis_r + 2.0 * (a + c))
    pair(3, jy, yy, axis_r + 2.0 * (a + b))
    pair(5, jz, zz, axis_r + 2.0 * (b + c))
    for i, u, even in ((7, jx + jy, plane_r - a), (9, jx - jy, plane_r - a), (11, jx + jz, plane_r - c),
                       (13, jx - jz, plane_r - c), (15, jy + jz, plane_r - b), (17, jy - jz, plane_r - b)):
        pair(i, u, u * u, even)
    return out


def pull(own, source, y_row):
    row = lax.broadcasted_iota(jnp.int32, (YS, ZS), 0)
    mine = [own(i) for i in range(19)]
    out = [mine[0]]
    for i in range(1, 19):
        cx, cy, cz = VELOCITIES[i]
        v = source(i)
        if cy == 1:
            v = jnp.where(row == 0, y_row(i), pltpu.roll(v, 1, 0))
        elif cy == -1:
            v = jnp.where(row == YS - 1, y_row(i), pltpu.roll(v, YS - 1, 0))
        if cz:
            v = pltpu.roll(v, cz % ZS, 1)
        reflected = mine[OPPOSITE[i]]
        v = jnp.where(v < HALF_BIG, v, reflected)
        out.append(jnp.where(v > -HALF_BIG, v, 2.0 * WALL_DENSITY * WEIGHTS[i] - reflected))
    return out


def fetch(hbm, vmem, sem):
    return [
        pltpu.make_async_copy(
            hbm.at[:, pl.ds(c * CHUNK, CHUNK)], vmem.at[:, pl.ds(1 + c * CHUNK, CHUNK)], sem.at[c]
        )
        for c in range(CHUNKS)
    ]


def place_x_halo(f, xlo, xhi):
    first = lax.axis_index("slab") == 0
    last = lax.axis_index("slab") == lax.axis_size("slab") - 1
    for k in range(5):
        f[X_UP[k], 0] = jnp.where(first, BIG, xlo[k])
        f[X_DOWN[k], XS + 1] = jnp.where(last, BIG, xhi[k])


def y_rows(inner, outer, x):
    first = lax.axis_index("blk") == 0
    last = lax.axis_index("blk") == lax.axis_size("blk") - 1
    even = lax.axis_index("blk") % 2 == 0

    def y_row(i):
        at = x + 1 - VELOCITIES[i][0]
        k = Y_UP.index(i) if i in Y_UP else Y_DOWN.index(i)
        a, b = inner[k, pl.ds(at, 1), :], outer[k, pl.ds(at, 1), :]
        if i in Y_UP:
            return jnp.where(first, BIG, jnp.where(even, b, a))
        return jnp.where(last, BIG, jnp.where(even, a, b))

    return y_row


def x_edges_kernel(pops, mark, xup, xdn, planes, sem):
    copies = []
    for k in range(5):
        copies.append(pltpu.make_async_copy(pops.at[X_UP[k], XS - 1], planes.at[k], sem.at[k]))
        copies.append(pltpu.make_async_copy(pops.at[X_DOWN[k], 0], planes.at[5 + k], sem.at[5 + k]))
    for copy in copies:
        copy.start()
    for copy in copies:
        copy.wait()
    for k in range(5):
        for out, at, m in ((xup, k, mark[1]), (xdn, 5 + k, mark[0])):
            out[k] = jnp.where(m == 0.0, planes[at], m)


def y_edges_kernel(pops, mark, yup, ydn, tiles, sem):
    copies = []
    for k in range(5):
        copies.append(pltpu.make_async_copy(pops.at[Y_UP[k], :, 8:16], tiles.at[k], sem.at[k]))
        copies.append(pltpu.make_async_copy(pops.at[Y_DOWN[k], :, 0:8], tiles.at[5 + k], sem.at[5 + k]))
    for copy in copies:
        copy.start()
    for copy in copies:
        copy.wait()
    for out, first, y in ((yup, 0, 7), (ydn, 5, 0)):
        m = mark[:, y + (8 if first == 0 else 0), :]
        for k in range(5):
            out[k, 1 : XS + 1, :] = jnp.where(m == 0.0, tiles[first + k, :, y, :], m)


def step_one_kernel(pops, mark, xlo, xhi, inner, outer, out, xup, xdn, yup, ydn, f, sem_in):
    copies = fetch(pops, f, sem_in)
    for copy in copies:
        copy.start()
    place_x_halo(f, xlo, xhi)
    def plane(x, carry):
        marked = {
            0: mark[x],
            1: jnp.where(x == 0, 0.0, mark[jnp.maximum(x - 1, 0)]),
            -1: jnp.where(x == XS - 1, 0.0, mark[jnp.minimum(x + 1, XS - 1)]),
        }

        def source(i):
            c = VELOCITIES[i][0]
            return jnp.where(marked[c] == 0.0, f[i, x + 1 - c], marked[c])

        pulled = pull(lambda i: f[i, x + 1], source, y_rows(inner, outer, x))
        new = collide(pulled)
        here = marked[0]
        for i in range(19):
            value = jnp.where(here == 0.0, new[i], here)
            out[i, x] = value
            if i in Y_UP:
                yup[Y_UP.index(i), pl.ds(x + 1, 1), :] = value[YS - 1 : YS]
            if i in Y_DOWN:
                ydn[Y_DOWN.index(i), pl.ds(x + 1, 1), :] = value[0:1]
        return carry

    copies[0].wait()
    for c in range(CHUNKS):
        if c + 1 < CHUNKS:
            copies[c + 1].wait()
        lax.fori_loop(c * CHUNK, (c + 1) * CHUNK, plane, 0, unroll=2)
    for k in range(5):
        xup[k] = out[X_UP[k], XS - 1]
        xdn[k] = out[X_DOWN[k], 0]


def step_two_kernel(owners, f, xlo, xhi, inner, outer, outgoing, buf, absent, sem_absent, sem_out):
    absent[...] = jnp.full((8, ZS), -1.0, jnp.float32)
    label_rows = pl.ds(BLOCK_ROWS, 8)
    clears = [
        pltpu.make_async_copy(absent, outgoing.at[p, label_rows], sem_absent.at[p])
        for p in range(outgoing.shape[0])
    ]
    for clear in clears:
        clear.start()
    for k in range(BLOCKS):
        at = (k // 8 * 8 + 7 - k % 8) * SLOT_ROWS + BLOCK_ROWS
        buf[at : at + 8, :] = jnp.full((8, ZS), float(k), jnp.float32)
    first = lax.axis_index("slab") == 0
    last = lax.axis_index("slab") == lax.axis_size("slab") - 1
    sub = lax.broadcasted_iota(jnp.int32, (8, ZS), 0)
    lane_block = lax.broadcasted_iota(jnp.int32, (8, ZS), 1) // 16
    pick = (lane_block + sub + 1) & 7

    def plane(x, carry):
        def source(i):
            at = x - VELOCITIES[i][0]
            if isinstance(at, int) and at < 0:
                return jnp.where(first, BIG, xlo[X_UP.index(i)])
            if isinstance(at, int) and at == XS:
                return jnp.where(last, BIG, xhi[X_DOWN.index(i)])
            return f[i, at]

        new = collide(pull(lambda i: f[i, x], source, y_rows(inner, outer, x)))
        fluid = jnp.abs(f[0, x]) < HALF_BIG
        base = x // 16 * (8 * SLOT_ROWS) + x % 16 // CHUNK * CHUNK_ROWS + x % CHUNK * 2
        tiles = []
        for i in range(19):
            value = jnp.where(fluid, new[i], 0.0)
            tiles += [(i * 2 * CHUNK + half, value[half * 8 : half * 8 + 8]) for half in range(2)]
        tiles = [(at, pltpu.roll(v, 0, 1, stride=16, stride_axis=0)) for at, v in tiles]
        tiles = [(at, jnp.take_along_axis(v, pick, axis=0)) for at, v in tiles]
        tiles = [(at, pltpu.roll(v, 16, 1, stride=16, stride_axis=0)) for at, v in tiles]
        for at, v in tiles:
            buf[pl.ds(base + at, 8, stride=SLOT_ROWS), :] = v
        return carry

    outs = []
    for c in range(CHUNKS):
        if c in (0, CHUNKS - 1):
            for x in range(c * CHUNK, (c + 1) * CHUNK):
                plane(x, 0)
        else:
            lax.fori_loop(c * CHUNK, (c + 1) * CHUNK, plane, 0, unroll=2)
        if c == 0:
            for clear in clears:
                clear.wait()
        part = c % 4
        rows = CHUNK_ROWS if part < 3 else CHUNK_ROWS + 8
        for k in range(c // 4 * 8, c // 4 * 8 + 8):
            at = (k // 8 * 8 + 7 - k % 8) * SLOT_ROWS + part * CHUNK_ROWS
            outs.append(
                pltpu.make_async_copy(
                    buf.at[pl.ds(at, rows)],
                    outgoing.at[owners[k], pl.ds(part * CHUNK_ROWS, rows)],
                    sem_out.at[k * 4 + part],
                )
            )
            outs[-1].start()
    for copy in outs:
        copy.wait()


def place_kernel(incoming, out, labels, blocks, res, sem_label, sem_in, sem_out):
    peers = incoming.shape[0]
    copy = pltpu.make_async_copy(incoming.at[:, pl.ds(BLOCK_ROWS, 8)], labels, sem_label)
    copy.start()
    copy.wait()
    lane = lax.broadcasted_iota(jnp.int32, (1, ZS), 1)
    slot = lane.astype(jnp.float32)
    found = jnp.zeros((1, ZS), jnp.int32)
    for p in range(peers):
        found += jnp.where(labels[p, 7:8, :] == slot, p, 0)
    ins = []
    for k in range(BLOCKS):
        source = jnp.clip(jnp.sum(jnp.where(lane == k, found, 0)), 0, peers - 1)
        ins.append(
            pltpu.make_async_copy(
                incoming.at[source], blocks.at[pl.ds(k * SLOT_ROWS, SLOT_ROWS)], sem_in.at[k]
            )
        )
        ins[-1].start()
    outs = []
    for h in range(2):
        for k in range(8):
            ins[h * 8 + k].wait()

        def channel(i, carry):
            for j in range(32):
                at = h * 8 * SLOT_ROWS + j // 8 * CHUNK_ROWS + i * 8 + j % 8
                res[i, h * 8 : h * 8 + 8, j * 128 : (j + 1) * 128] = blocks[
                    pl.ds(at, 8, stride=SLOT_ROWS), :
                ]
            return carry

        for part, (low, high) in enumerate(((0, 5), (5, 10), (10, 15), (15, 19))):
            lax.fori_loop(low, high, channel, 0)
            at = (pl.ds(low, high - low), pl.ds(h * 8, 8))
            outs.append(pltpu.make_async_copy(res.at[at], out.at[at], sem_out.at[h * 4 + part]))
            outs[-1].start()
    for copy in outs:
        copy.wait()


VMEM = pl.BlockSpec(memory_space=pltpu.VMEM)
ANY = pl.BlockSpec(memory_space=pl.ANY)
SMEM = pl.BlockSpec(memory_space=pltpu.SMEM)


def sds(*shape):
    return jax.ShapeDtypeStruct(shape, jnp.float32)


def params(mib=48):
    return pltpu.CompilerParams(vmem_limit_bytes=mib * 1024 * 1024)


EDGES = (sds(5, YS, ZS), sds(5, YS, ZS), sds(5, HALO_ROWS, ZS), sds(5, HALO_ROWS, ZS))


def edges(kernel, name, edge, scratch, pops, mark):
    return pl.pallas_call(
        kernel,
        out_shape=(edge, edge),
        in_specs=[ANY, VMEM],
        out_specs=(VMEM, VMEM),
        scratch_shapes=[pltpu.VMEM(scratch, jnp.float32), pltpu.SemaphoreType.DMA((10,))],
        compiler_params=params(50),
        cost_estimate=pl.CostEstimate(flops=10**6, bytes_accessed=3 * 10**6, transcendentals=0),
        name=name,
    )(pops, mark)


def step_one(pops, mark, halo):
    return pl.pallas_call(
        step_one_kernel,
        out_shape=(sds(19, XS, YS, ZS), *EDGES),
        in_specs=[ANY] + [VMEM] * 5,
        out_specs=(VMEM,) * 5,
        scratch_shapes=[
            pltpu.VMEM((19, XS + 2, YS, ZS), jnp.float32),
            pltpu.SemaphoreType.DMA((CHUNKS,)),
        ],
        compiler_params=params(),
        name="step_one",
    )(pops, mark, *halo)


def step_two(owners, f1, halo, peers):
    return pl.pallas_call(
        step_two_kernel,
        out_shape=sds(peers, SLOT_ROWS, ZS),
        in_specs=[SMEM] + [VMEM] * 5,
        out_specs=ANY,
        scratch_shapes=[
            pltpu.VMEM((BLOCKS * SLOT_ROWS, ZS), jnp.float32),
            pltpu.VMEM((8, ZS), jnp.float32),
            pltpu.SemaphoreType.DMA((peers,)),
            pltpu.SemaphoreType.DMA((BLOCKS * 4,)),
        ],
        compiler_params=params(),
        name="step_two",
    )(owners, f1, *halo)


def place(incoming):
    peers = incoming.shape[0]
    return pl.pallas_call(
        place_kernel,
        out_shape=sds(19, BLOCKS, 4096),
        in_specs=[ANY],
        out_specs=ANY,
        scratch_shapes=[
            pltpu.VMEM((peers, 8, ZS), jnp.float32),
            pltpu.VMEM((BLOCKS * SLOT_ROWS, ZS), jnp.float32),
            pltpu.VMEM((19, BLOCKS, 4096), jnp.float32),
            pltpu.SemaphoreType.DMA,
            pltpu.SemaphoreType.DMA((BLOCKS,)),
            pltpu.SemaphoreType.DMA((8,)),
        ],
        compiler_params=params(),
        name="place",
    )(incoming)


def shift(value, axis, up):
    count = lax.axis_size(axis)
    steps = [(i, (i + 1) % count) if up else ((i + 1) % count, i) for i in range(count)]
    return lax.ppermute(value, axis, steps)


def exchange(x_planes, yup, ydn):
    xlo, xhi = x_planes
    first = lax.axis_index("slab") == 0
    last = lax.axis_index("slab") == lax.axis_size("slab") - 1
    row = jnp.arange(HALO_ROWS)[:, None]

    def corners(rows, lo_channel, hi_channel, y, channels):
        parts = []
        for k, i in enumerate(channels):
            part = rows[k]
            if i == lo_channel:
                part = jnp.where(row == 0, jnp.where(first, BIG, xlo[X_UP.index(i), y]), part)
            if i == hi_channel:
                part = jnp.where(row == XS + 1, jnp.where(last, BIG, xhi[X_DOWN.index(i), y]), part)
            parts.append(part)
        return jnp.stack(parts)

    yup = corners(yup, 7, 10, YS - 1, Y_UP)
    ydn = corners(ydn, 9, 8, 0, Y_DOWN)
    even = lax.axis_index("blk") % 2 == 0
    count = lax.axis_size("blk")
    across = [((i + 1) ^ 1) - 1 for i in range(count)]
    across = [(i, j if 0 <= j < count else i) for i, j in enumerate(across)]
    outer = lax.ppermute(jnp.where(even, ydn, yup), "blk", across)
    inner = lax.ppermute(jnp.where(even, yup, ydn), "blk", [(i, i ^ 1) for i in range(count)])
    return xlo, xhi, inner, outer


def per_device(populations, solid, wetting, dest):
    peers = lax.axis_size("blk")

    def marks(solid, wetting):
        return jnp.where(solid == 1, jnp.where(wetting == 1, -BIG, BIG), 0.0)

    def ends(kinds):
        return jnp.stack([kinds[0], kinds[XS - 1]])

    def x_exchange(xup, xdn):
        return shift(xup, "slab", True), shift(xdn, "slab", False)

    x_marks = marks(ends(solid), ends(wetting))
    x_planes = x_exchange(
        *edges(x_edges_kernel, "x_edges", sds(5, YS, ZS), (10, YS, ZS), populations, x_marks)
    )
    mark = marks(solid, wetting)
    rows = edges(y_edges_kernel, "y_edges", sds(5, HALO_ROWS, ZS), (10, XS, 8, ZS), populations, mark)
    f1, xup, xdn, yup, ydn = step_one(populations, mark, exchange(x_planes, *rows))
    outgoing = step_two(dest[0] // BLOCKS, f1, exchange(x_exchange(xup, xdn), yup, ydn), peers)
    incoming = lax.all_to_all(outgoing, "blk", split_axis=0, concat_axis=0, tiled=True)
    return place(incoming).transpose(1, 0, 2)


def solution(mesh):
    in_specs = (
        P(None, "slab", "blk", None),
        P("slab", "blk", None),
        P("slab", "blk", None),
        P("slab", "blk"),
    )
    out_specs = P(("slab", "blk"), None, None)
    return jax.shard_map(
        per_device, mesh=mesh, in_specs=in_specs, out_specs=out_specs, check_vma=False
    )
```

```python
import functools

import jax
import jax.numpy as jnp
import numpy as np
from jax import lax
from jax.experimental import pallas as pl
from jax.experimental.pallas import tpu as pltpu
from jax.sharding import PartitionSpec as P

VELOCITIES = [
    (0, 0, 0), (1, 0, 0), (-1, 0, 0), (0, 1, 0), (0, -1, 0), (0, 0, 1), (0, 0, -1),
    (1, 1, 0), (-1, -1, 0), (1, -1, 0), (-1, 1, 0), (1, 0, 1), (-1, 0, -1), (1, 0, -1),
    (-1, 0, 1), (0, 1, 1), (0, -1, -1), (0, 1, -1), (0, -1, 1),
]
OPPOSITE = [0, 2, 1, 4, 3, 6, 5, 8, 7, 10, 9, 12, 11, 14, 13, 16, 15, 18, 17]
WEIGHTS = [1.0 / 3.0] + [1.0 / 18.0] * 6 + [1.0 / 36.0] * 12
WALL_DENSITY = 1.2
BIG = 1e30
HALF_BIG = 1e29

X_UP = [i for i in range(19) if VELOCITIES[i][0] == 1]
X_DOWN = [i for i in range(19) if VELOCITIES[i][0] == -1]
Y_UP = [i for i in range(19) if VELOCITIES[i][1] == 1]
Y_DOWN = [i for i in range(19) if VELOCITIES[i][1] == -1]

XS, YS, ZS = 32, 16, 128
HALO_ROWS = 40
CHUNK = 4
CHUNKS = XS // CHUNK
FETCHES = ((0, 2), (2, 4)) + tuple((x, x + CHUNK) for x in range(4, XS, CHUNK))
BLOCKS = 16
BLOCK_ROWS = 19 * 32
SLOT_ROWS = BLOCK_ROWS + 8
CHUNK_ROWS = 19 * 2 * CHUNK


def collide(f):
    s, d = {}, {}
    for i in range(1, 19, 2):
        s[i] = f[i] + f[i + 1]
        d[i] = f[i] - f[i + 1]
    sxy, sxz, syz = s[7] + s[9], s[11] + s[13], s[15] + s[17]
    sx, sy, sz = s[1], s[3], s[5]
    rho = f[0] + (sx + sy) + (sz + sxy) + (sxz + syz)
    jx = d[1] + (d[7] + d[9]) + (d[11] + d[13])
    jy = d[3] + (d[7] - d[9]) + (d[15] + d[17])
    jz = d[5] + (d[11] - d[13]) + (d[15] - d[17])
    xx, yy, zz = jx * jx, jy * jy, jz * jz
    r = rho - 1.5 * (xx + yy + zz)
    tx, ty, tz = 2.0 * sx + 0.5 * xx, 2.0 * sy + 0.5 * yy, 2.0 * sz + 0.5 * zz
    base = 4.0 * f[0] - r
    qxy = (sxy - tx) + (base - ty + (xx + yy))
    qyz = (syz - ty) + (base - tz + (yy + zz))
    qxz = (sxz - tx) + (base - tz + (xx + zz))
    mean = (qxy + qyz + qxz) * (2.0 / 7.0)
    scale = 0.15 / 12.0
    a, b, c = (qxy - mean) * scale, (qyz - mean) * scale, (qxz - mean) * scale
    out = [None] * 19
    out[0] = -0.25 * f[0] + (1.25 / 3.0) * r - 4.0 * (a + b + c)
    axis_r = (1.25 / 18.0) * r
    plane_r = (1.25 / 36.0) * r

    def pair(i, along, square, even):
        w = WEIGHTS[i]
        e = even - 0.125 * s[i] + (1.25 * 4.5 * w) * square
        o = (1.6 * 3.0 * w) * along - 0.3 * d[i]
        out[i] = e + o
        out[i + 1] = e - o

    pair(1, jx, xx, axis_r + 2.0 * (a + c))
    pair(3, jy, yy, axis_r + 2.0 * (a + b))
    pair(5, jz, zz, axis_r + 2.0 * (b + c))
    for i, u, even in ((7, jx + jy, plane_r - a), (9, jx - jy, plane_r - a), (11, jx + jz, plane_r - c),
                       (13, jx - jz, plane_r - c), (15, jy + jz, plane_r - b), (17, jy - jz, plane_r - b)):
        pair(i, u, u * u, even)
    return out


def pull(own, source, y_row):
    row = lax.broadcasted_iota(jnp.int32, (YS, ZS), 0)
    mine = [own(i) for i in range(19)]
    out = [mine[0]]
    for i in range(1, 19):
        cx, cy, cz = VELOCITIES[i]
        v = source(i)
        if cy == 1:
            v = jnp.where(row == 0, y_row(i), pltpu.roll(v, 1, 0))
        elif cy == -1:
            v = jnp.where(row == YS - 1, y_row(i), pltpu.roll(v, YS - 1, 0))
        if cz:
            v = pltpu.roll(v, cz % ZS, 1)
        reflected = mine[OPPOSITE[i]]
        v = jnp.where(v < HALF_BIG, v, reflected)
        out.append(jnp.where(v > -HALF_BIG, v, 2.0 * WALL_DENSITY * WEIGHTS[i] - reflected))
    return out


def fetch(hbm, vmem, sem):
    return [
        pltpu.make_async_copy(
            hbm.at[:, pl.ds(low, high - low)], vmem.at[:, pl.ds(1 + low, high - low)], sem.at[c]
        )
        for c, (low, high) in enumerate(FETCHES)
    ]


def place_x_halo(f, xlo, xhi):
    first = lax.axis_index("slab") == 0
    last = lax.axis_index("slab") == lax.axis_size("slab") - 1
    for k in range(5):
        f[X_UP[k], 0] = jnp.where(first, BIG, xlo[k])
        f[X_DOWN[k], XS + 1] = jnp.where(last, BIG, xhi[k])


def y_rows(inner, outer, x):
    first = lax.axis_index("blk") == 0
    last = lax.axis_index("blk") == lax.axis_size("blk") - 1
    even = lax.axis_index("blk") % 2 == 0

    def y_row(i):
        at = x + 1 - VELOCITIES[i][0]
        k = Y_UP.index(i) if i in Y_UP else Y_DOWN.index(i)
        a, b = inner[k, pl.ds(at, 1), :], outer[k, pl.ds(at, 1), :]
        if i in Y_UP:
            return jnp.where(first, BIG, jnp.where(even, b, a))
        return jnp.where(last, BIG, jnp.where(even, a, b))

    return y_row


def x_edges_kernel(pops, mark, xup, xdn, planes, sem):
    copies = []
    for k in range(5):
        copies.append(pltpu.make_async_copy(pops.at[X_UP[k], XS - 1], planes.at[k], sem.at[k]))
        copies.append(pltpu.make_async_copy(pops.at[X_DOWN[k], 0], planes.at[5 + k], sem.at[5 + k]))
    for copy in copies:
        copy.start()
    for copy in copies:
        copy.wait()
    for k in range(5):
        for out, at, m in ((xup, k, mark[1]), (xdn, 5 + k, mark[0])):
            out[k] = jnp.where(m == 0.0, planes[at], m)


def y_edges_kernel(pops, mark, yup, ydn, tiles, sem):
    copies = []
    for k in range(5):
        copies.append(pltpu.make_async_copy(pops.at[Y_UP[k], :, 8:16], tiles.at[k], sem.at[k]))
        copies.append(pltpu.make_async_copy(pops.at[Y_DOWN[k], :, 0:8], tiles.at[5 + k], sem.at[5 + k]))
    for copy in copies:
        copy.start()
    for copy in copies:
        copy.wait()
    for out, first, y in ((yup, 0, 7), (ydn, 5, 0)):
        m = mark[:, y + (8 if first == 0 else 0), :]
        for k in range(5):
            out[k, 1 : XS + 1, :] = jnp.where(m == 0.0, tiles[first + k, :, y, :], m)


def step_one_kernel(pops, mark, xlo, xhi, inner, outer, out, xup, xdn, yup, ydn, f, sem_in):
    copies = fetch(pops, f, sem_in)
    for copy in copies:
        copy.start()
    place_x_halo(f, xlo, xhi)
    def plane(x, carry):
        marked = {
            0: mark[x],
            1: jnp.where(x == 0, 0.0, mark[jnp.maximum(x - 1, 0)]),
            -1: jnp.where(x == XS - 1, 0.0, mark[jnp.minimum(x + 1, XS - 1)]),
        }

        def source(i):
            c = VELOCITIES[i][0]
            return jnp.where(marked[c] == 0.0, f[i, x + 1 - c], marked[c])

        pulled = pull(lambda i: f[i, x + 1], source, y_rows(inner, outer, x))
        new = collide(pulled)
        here = marked[0]
        for i in range(19):
            value = jnp.where(here == 0.0, new[i], here)
            out[i, x] = value
            if i in Y_UP:
                yup[Y_UP.index(i), pl.ds(x + 1, 1), :] = value[YS - 1 : YS]
            if i in Y_DOWN:
                ydn[Y_DOWN.index(i), pl.ds(x + 1, 1), :] = value[0:1]
        return carry

    copies[0].wait()
    for c, (low, high) in enumerate(FETCHES):
        if c + 1 < len(FETCHES):
            copies[c + 1].wait()
        lax.fori_loop(low, high, plane, 0, unroll=2)
    for k in range(5):
        xup[k] = out[X_UP[k], XS - 1]
        xdn[k] = out[X_DOWN[k], 0]


def step_two_kernel(owners, f, xlo, xhi, inner, outer, outgoing, buf, absent, sem_absent, sem_out):
    absent[...] = jnp.full((8, ZS), -1.0, jnp.float32)
    label_rows = pl.ds(BLOCK_ROWS, 8)
    clears = [
        pltpu.make_async_copy(absent, outgoing.at[p, label_rows], sem_absent.at[p])
        for p in range(outgoing.shape[0])
    ]
    for clear in clears:
        clear.start()
    for k in range(BLOCKS):
        at = (k // 8 * 8 + 7 - k % 8) * SLOT_ROWS + BLOCK_ROWS
        buf[at : at + 8, :] = jnp.full((8, ZS), float(k), jnp.float32)
    first = lax.axis_index("slab") == 0
    last = lax.axis_index("slab") == lax.axis_size("slab") - 1
    sub = lax.broadcasted_iota(jnp.int32, (8, ZS), 0)
    lane_block = lax.broadcasted_iota(jnp.int32, (8, ZS), 1) // 16
    pick = (lane_block + sub + 1) & 7

    def plane(x, carry):
        def source(i):
            at = x - VELOCITIES[i][0]
            if isinstance(at, int) and at < 0:
                return jnp.where(first, BIG, xlo[X_UP.index(i)])
            if isinstance(at, int) and at == XS:
                return jnp.where(last, BIG, xhi[X_DOWN.index(i)])
            return f[i, at]

        new = collide(pull(lambda i: f[i, x], source, y_rows(inner, outer, x)))
        fluid = jnp.abs(f[0, x]) < HALF_BIG
        base = x // 16 * (8 * SLOT_ROWS) + x % 16 // CHUNK * CHUNK_ROWS + x % CHUNK * 2
        tiles = []
        for i in range(19):
            value = jnp.where(fluid, new[i], 0.0)
            tiles += [(i * 2 * CHUNK + half, value[half * 8 : half * 8 + 8]) for half in range(2)]
        tiles = [(at, pltpu.roll(v, 0, 1, stride=16, stride_axis=0)) for at, v in tiles]
        tiles = [(at, jnp.take_along_axis(v, pick, axis=0)) for at, v in tiles]
        tiles = [(at, pltpu.roll(v, 16, 1, stride=16, stride_axis=0)) for at, v in tiles]
        for at, v in tiles:
            buf[pl.ds(base + at, 8, stride=SLOT_ROWS), :] = v
        return carry

    outs = []
    for c in range(CHUNKS):
        if c in (0, CHUNKS - 1):
            for x in range(c * CHUNK, (c + 1) * CHUNK):
                plane(x, 0)
        else:
            lax.fori_loop(c * CHUNK, (c + 1) * CHUNK, plane, 0, unroll=2)
        if c == 0:
            for clear in clears:
                clear.wait()
        part = c % 4
        rows = CHUNK_ROWS if part < 3 else CHUNK_ROWS + 8
        for k in range(c // 4 * 8, c // 4 * 8 + 8):
            at = (k // 8 * 8 + 7 - k % 8) * SLOT_ROWS + part * CHUNK_ROWS
            outs.append(
                pltpu.make_async_copy(
                    buf.at[pl.ds(at, rows)],
                    outgoing.at[owners[k], pl.ds(part * CHUNK_ROWS, rows)],
                    sem_out.at[k * 4 + part],
                )
            )
            outs[-1].start()
    for copy in outs:
        copy.wait()


def place_kernel(incoming, out, labels, blocks, res, sem_label, sem_in, sem_out):
    peers = incoming.shape[0]
    copy = pltpu.make_async_copy(incoming.at[:, pl.ds(BLOCK_ROWS, 8)], labels, sem_label)
    copy.start()
    copy.wait()
    lane = lax.broadcasted_iota(jnp.int32, (1, ZS), 1)
    slot = lane.astype(jnp.float32)
    found = jnp.zeros((1, ZS), jnp.int32)
    for p in range(peers):
        found += jnp.where(labels[p, 7:8, :] == slot, p, 0)
    ins = []
    for k in range(BLOCKS):
        source = jnp.clip(jnp.sum(jnp.where(lane == k, found, 0)), 0, peers - 1)
        ins.append(
            pltpu.make_async_copy(
                incoming.at[source], blocks.at[pl.ds(k * SLOT_ROWS, SLOT_ROWS)], sem_in.at[k]
            )
        )
        ins[-1].start()
    outs = []
    for h in range(2):
        for k in range(8):
            ins[h * 8 + k].wait()

        def channel(i, carry):
            for j in range(32):
                at = h * 8 * SLOT_ROWS + j // 8 * CHUNK_ROWS + i * 8 + j % 8
                res[i, h * 8 : h * 8 + 8, j * 128 : (j + 1) * 128] = blocks[
                    pl.ds(at, 8, stride=SLOT_ROWS), :
                ]
            return carry

        for part, (low, high) in enumerate(((0, 5), (5, 10), (10, 15), (15, 19))):
            lax.fori_loop(low, high, channel, 0)
            at = (pl.ds(low, high - low), pl.ds(h * 8, 8))
            outs.append(pltpu.make_async_copy(res.at[at], out.at[at], sem_out.at[h * 4 + part]))
            outs[-1].start()
    for copy in outs:
        copy.wait()


VMEM = pl.BlockSpec(memory_space=pltpu.VMEM)
ANY = pl.BlockSpec(memory_space=pl.ANY)
SMEM = pl.BlockSpec(memory_space=pltpu.SMEM)


def sds(*shape):
    return jax.ShapeDtypeStruct(shape, jnp.float32)


def params(mib=48):
    return pltpu.CompilerParams(vmem_limit_bytes=mib * 1024 * 1024)


EDGES = (sds(5, YS, ZS), sds(5, YS, ZS), sds(5, HALO_ROWS, ZS), sds(5, HALO_ROWS, ZS))


def edges(kernel, name, edge, scratch, pops, mark):
    return pl.pallas_call(
        kernel,
        out_shape=(edge, edge),
        in_specs=[ANY, VMEM],
        out_specs=(VMEM, VMEM),
        scratch_shapes=[pltpu.VMEM(scratch, jnp.float32), pltpu.SemaphoreType.DMA((10,))],
        compiler_params=params(50),
        cost_estimate=pl.CostEstimate(flops=10**6, bytes_accessed=3 * 10**6, transcendentals=0),
        name=name,
    )(pops, mark)


def step_one(pops, mark, halo):
    return pl.pallas_call(
        step_one_kernel,
        out_shape=(sds(19, XS, YS, ZS), *EDGES),
        in_specs=[ANY] + [VMEM] * 5,
        out_specs=(VMEM,) * 5,
        scratch_shapes=[
            pltpu.VMEM((19, XS + 2, YS, ZS), jnp.float32),
            pltpu.SemaphoreType.DMA((len(FETCHES),)),
        ],
        compiler_params=params(),
        name="step_one",
    )(pops, mark, *halo)


def step_two(owners, f1, halo, peers):
    return pl.pallas_call(
        step_two_kernel,
        out_shape=sds(peers, SLOT_ROWS, ZS),
        in_specs=[SMEM] + [VMEM] * 5,
        out_specs=ANY,
        scratch_shapes=[
            pltpu.VMEM((BLOCKS * SLOT_ROWS, ZS), jnp.float32),
            pltpu.VMEM((8, ZS), jnp.float32),
            pltpu.SemaphoreType.DMA((peers,)),
            pltpu.SemaphoreType.DMA((BLOCKS * 4,)),
        ],
        compiler_params=params(),
        name="step_two",
    )(owners, f1, *halo)


def place(incoming):
    peers = incoming.shape[0]
    return pl.pallas_call(
        place_kernel,
        out_shape=sds(19, BLOCKS, 4096),
        in_specs=[ANY],
        out_specs=ANY,
        scratch_shapes=[
            pltpu.VMEM((peers, 8, ZS), jnp.float32),
            pltpu.VMEM((BLOCKS * SLOT_ROWS, ZS), jnp.float32),
            pltpu.VMEM((19, BLOCKS, 4096), jnp.float32),
            pltpu.SemaphoreType.DMA,
            pltpu.SemaphoreType.DMA((BLOCKS,)),
            pltpu.SemaphoreType.DMA((8,)),
        ],
        compiler_params=params(),
        name="place",
    )(incoming)


def shift(value, axis, up):
    count = lax.axis_size(axis)
    steps = [(i, (i + 1) % count) if up else ((i + 1) % count, i) for i in range(count)]
    return lax.ppermute(value, axis, steps)


def exchange(x_planes, yup, ydn):
    xlo, xhi = x_planes
    first = lax.axis_index("slab") == 0
    last = lax.axis_index("slab") == lax.axis_size("slab") - 1
    row = jnp.arange(HALO_ROWS)[:, None]

    def corners(rows, lo_channel, hi_channel, y, channels):
        parts = []
        for k, i in enumerate(channels):
            part = rows[k]
            if i == lo_channel:
                part = jnp.where(row == 0, jnp.where(first, BIG, xlo[X_UP.index(i), y]), part)
            if i == hi_channel:
                part = jnp.where(row == XS + 1, jnp.where(last, BIG, xhi[X_DOWN.index(i), y]), part)
            parts.append(part)
        return jnp.stack(parts)

    yup = corners(yup, 7, 10, YS - 1, Y_UP)
    ydn = corners(ydn, 9, 8, 0, Y_DOWN)
    even = lax.axis_index("blk") % 2 == 0
    count = lax.axis_size("blk")
    across = [((i + 1) ^ 1) - 1 for i in range(count)]
    across = [(i, j if 0 <= j < count else i) for i, j in enumerate(across)]
    outer = lax.ppermute(jnp.where(even, ydn, yup), "blk", across)
    inner = lax.ppermute(jnp.where(even, yup, ydn), "blk", [(i, i ^ 1) for i in range(count)])
    return xlo, xhi, inner, outer


def per_device(populations, solid, wetting, dest):
    peers = lax.axis_size("blk")

    def marks(solid, wetting):
        return jnp.where(solid == 1, jnp.where(wetting == 1, -BIG, BIG), 0.0)

    def ends(kinds):
        return jnp.stack([kinds[0], kinds[XS - 1]])

    def x_exchange(xup, xdn):
        return shift(xup, "slab", True), shift(xdn, "slab", False)

    x_marks = marks(ends(solid), ends(wetting))
    x_planes = x_exchange(
        *edges(x_edges_kernel, "x_edges", sds(5, YS, ZS), (10, YS, ZS), populations, x_marks)
    )
    mark = marks(solid, wetting)
    rows = edges(y_edges_kernel, "y_edges", sds(5, HALO_ROWS, ZS), (10, XS, 8, ZS), populations, mark)
    f1, xup, xdn, yup, ydn = step_one(populations, mark, exchange(x_planes, *rows))
    outgoing = step_two(dest[0] // BLOCKS, f1, exchange(x_exchange(xup, xdn), yup, ydn), peers)
    incoming = lax.all_to_all(outgoing, "blk", split_axis=0, concat_axis=0, tiled=True)
    return place(incoming).transpose(1, 0, 2)


def solution(mesh):
    in_specs = (
        P(None, "slab", "blk", None),
        P("slab", "blk", None),
        P("slab", "blk", None),
        P("slab", "blk"),
    )
    out_specs = P(("slab", "blk"), None, None)
    return jax.shard_map(
        per_device, mesh=mesh, in_specs=in_specs, out_specs=out_specs, check_vma=False
    )
```
